32 devices in a mesh: ctx: 4 (over y, core), head: 8 (over z, x).
Axes of the slice: x: 2, y: 2, z: 4, core: 2. Of those that a mesh axis runs over, the one named last changes fastest.
Arguments:
- tokens: bfloat16 [4096, 2048], P('ctx', 'head'), may hold values from -6 to 6
- beta: float32 [4096, 8], P('ctx', 'head'), may hold values from 0 to 2
- w_query: bfloat16 [2048, 1024], P(None, 'head'), may hold values from -0.125 to 0.125
- w_key: bfloat16 [2048, 1024], P(None, 'head'), may hold values from -0.125 to 0.125
- w_value: bfloat16 [2048, 1024], P(None, 'head'), may hold values from -0.125 to 0.125
- gain: float32 [128], replicated, may hold values from 0.25 to 1.75
- w_out: bfloat16 [1024, 2048], P('head'), may hold values from -0.1875 to 0.1875
Outputs:
- mixed: bfloat16 [4096, 2048], P(('ctx', 'head'))
The draws below stay inside these ranges and needn't reach their ends.
All inputs are finite; a program needn't handle non-finite values.
Results may differ from the reference program's by a relative error of at most 0.023.
Values may be sent and summed in bfloat16 or wider, within the bound.
A program may use at most 64 MiB of HBM per device.

```python
import jax
import jax.numpy as jnp
from jax import lax

D = 2048
DK = 128
BLOCK = 64
H = 8
SLAB_TOKENS = 4096


def draw_beta(key, part):
    key = jax.random.fold_in(key, 11)
    gradual_key, quick_key, selection_key, jitter_key, spike_key = jax.random.split(key, 5)
    slow_rate = DK * jax.random.uniform(gradual_key, (H,), jnp.float32, 0.2, 1.0) / SLAB_TOKENS
    fast_rate = jax.random.uniform(quick_key, (H,), jnp.float32, 0.3, 0.8)
    ranking = jax.random.permutation(selection_key, H)
    fast_count = H // 2
    baseline_rate = jnp.where(ranking < fast_count, fast_rate, slow_rate)
    jitter_level = jax.random.uniform(jitter_key, (SLAB_TOKENS, H), jnp.float32, 0.5, 1.5)
    locations = jax.random.randint(spike_key, (8,), 0, SLAB_TOKENS)
    positions = jnp.arange(SLAB_TOKENS, dtype=jnp.int32)[:, None]
    spike_level = jnp.any(positions == locations[None, :], axis=1)
    value_rows = jnp.where(spike_level[:, None], 1.5, baseline_rate[None, :] * jitter_level)
    return value_rows.astype(jnp.float32)


def levels(rng, extent, cuts, smallest, high):
    level, own = 1.0, jax.random.fold_in(rng, 6)
    for dim, blocks in cuts:
        heights = jnp.exp(jax.random.uniform(jax.random.fold_in(own, dim), (blocks,), jnp.float32, smallest / len(cuts), high / len(cuts)))
        level = level * jnp.repeat(heights, extent[dim] // blocks).reshape([-1 if axis == dim else 1 for axis in range(len(extent))])
    return level


def centred(rng, dims, deviation, limit, cuts=(), kind=jnp.bfloat16):
    result = jax.random.normal(rng, dims, jnp.float32) * deviation
    if len(cuts) > 0:
        result = levels(rng, dims, cuts, -0.22, 0.18) * result
    return jnp.clip(result, min=-limit, max=limit).astype(kind)


def setup_inputs(seed: int = 0) -> dict:
    arg_keys = jax.random.split(jax.random.key(seed), 8)
    return {
        "tokens": centred(arg_keys[0], (SLAB_TOKENS, D), 1.0, 6.0, ((0, 4), (1, 8))),
        "beta": draw_beta(jax.random.fold_in(arg_keys[7], 71), 0),
        "w_query": centred(arg_keys[2], (D, H * DK), D ** -0.5, 0.125, ((1, 8),)),
        "w_key": centred(arg_keys[3], (D, H * DK), D ** -0.5, 0.125, ((1, 8),)),
        "w_value": centred(arg_keys[4], (D, H * DK), D ** -0.5, 0.125, ((1, 8),)),
        "gain": jnp.clip(1.0 + 0.15 * jax.random.normal(arg_keys[5], (DK,), jnp.float32), 0.25, 1.75),
        "w_out": centred(arg_keys[6], (H * DK, D), (H * DK) ** -0.5, 0.1875, ((0, 8),)),
    }


def matmul(left, right):
    return jnp.dot(left.astype(jnp.float32), right.astype(jnp.float32), precision=lax.Precision.HIGHEST, preferred_element_type=jnp.float32)

def unit_rows(matrix):
    return matrix * lax.rsqrt(lax.optimization_barrier(jnp.sum(matrix * matrix, axis=-1, keepdims=True)) + 1e-06)

def head_run(operands):
    queries, keys, value_rows, rates = operands
    count = queries.shape[0] // BLOCK
    blocked = (queries.reshape(count, BLOCK, DK), keys.reshape(count, BLOCK, DK), value_rows.reshape(count, BLOCK, DK), rates.reshape(count, BLOCK))

    def advance(memory_state, block_data):
        block_query, block_key, block_value, block_rate = block_data
        lower_tri = jnp.tril(block_rate[:, None] * matmul(block_key, block_key.T), -1) + jnp.eye(BLOCK, dtype=jnp.float32)
        key_factor = jax.scipy.linalg.solve_triangular(lower_tri, block_rate[:, None] * block_key, lower=True, unit_diagonal=True)
        value_factor = jax.scipy.linalg.solve_triangular(lower_tri, block_rate[:, None] * block_value, lower=True, unit_diagonal=True)
        written = value_factor - matmul(key_factor, memory_state.T)
        output_rows = matmul(block_query, memory_state.T) + matmul(jnp.tril(matmul(block_query, block_key.T)), written)
        memory_state = memory_state + matmul(written.T, block_key)
        return (memory_state, output_rows)
    _, outputs = lax.scan(advance, jnp.zeros((DK, DK), jnp.float32), blocked)
    return outputs.reshape(count * BLOCK, DK)

def reference(tokens, beta, w_query, w_key, w_value, gain, w_out):

    def project(weight):
        raw_proj = jnp.dot(tokens.astype(jnp.float32), weight.astype(jnp.float32), preferred_element_type=jnp.float32)
        return raw_proj.reshape(SLAB_TOKENS, H, DK).transpose(1, 0, 2)
    queries = unit_rows(jax.nn.silu(project(w_query)))
    keys = unit_rows(jax.nn.silu(project(w_key)))
    value_rows = project(w_value)
    recurrent = lax.map(head_run, (queries, keys, value_rows, beta.T))
    scale_inv = lax.rsqrt(lax.optimization_barrier(jnp.mean(recurrent * recurrent, axis=-1, keepdims=True)) + 1e-05)
    normed = (recurrent * scale_inv * gain).astype(jnp.bfloat16)
    normed = normed.transpose(1, 0, 2).reshape(SLAB_TOKENS, H * DK)
    return jnp.dot(normed.astype(jnp.float32), w_out.astype(jnp.float32), preferred_element_type=jnp.float32).astype(jnp.bfloat16)
```

```python
import functools

import jax
import jax.numpy as jnp
from jax import lax
from jax.experimental import pallas as pl
from jax.experimental.pallas import tpu as pltpu
from jax.sharding import PartitionSpec as P

DK = 128
CHUNK = 128
F32, BF16 = jnp.float32, jnp.bfloat16


def dot(left, right):
    return jnp.dot(left.astype(BF16), right.astype(BF16), preferred_element_type=F32)


def dot_nt(left, right):
    return lax.dot_general(
        left.astype(BF16), right.astype(BF16), (((1,), (1,)), ((), ())), preferred_element_type=F32
    )


def dot_tn(left, right):
    return lax.dot_general(
        left.astype(BF16), right.astype(BF16), (((0,), (0,)), ((), ())), preferred_element_type=F32
    )


def unit_silu(raw):
    act = raw / (1.0 + jnp.exp(-raw))
    return act * lax.rsqrt(jnp.sum(act * act, axis=-1, keepdims=True) + 1e-6)


def unit_lower_inverses(lowers):
    size = lowers[0].shape[0]
    row = lax.broadcasted_iota(jnp.int32, (size, size), 0)
    col = lax.broadcasted_iota(jnp.int32, (size, size), 1)
    inverses = None
    level = 0
    while (1 << level) < size:
        mask = (
            ((row >> (level + 1)) == (col >> (level + 1)))
            & (((row >> level) & 1) == 1)
            & (((col >> level) & 1) == 0)
        )
        parts = [jnp.where(mask, lower, 0.0) for lower in lowers]
        if inverses is None:
            eye = jnp.where(row == col, 1.0, 0.0)
            inverses = [eye - part for part in parts]
        else:
            halves = [dot(inverse, part) for inverse, part in zip(inverses, parts)]
            inverses = [
                inverse - dot(half, inverse) for inverse, half in zip(inverses, halves)
            ]
        level += 1
    return inverses


def shard_maps(raw, rates, emit):
    count = len(raw)
    row = lax.broadcasted_iota(jnp.int32, (CHUNK, CHUNK), 0)
    col = lax.broadcasted_iota(jnp.int32, (CHUNK, CHUNK), 1)
    queries = [unit_silu(raw[i][0]) for i in range(count)]
    keys = [unit_silu(raw[i][1]) for i in range(count)]
    lowers = [
        jnp.where(row > col, rates[i] * dot_nt(keys[i], keys[i]), 0.0) for i in range(count)
    ]
    inverses = unit_lower_inverses(lowers)
    factors = [
        dot(inverses[i], jnp.concatenate([rates[i] * keys[i], rates[i] * raw[i][2]], axis=1))
        for i in range(count)
    ]
    moves = [dot_tn(keys[i], factors[i]) for i in range(count)]
    reads = [
        dot(jnp.where(row >= col, dot_nt(queries[i], keys[i]), 0.0), factors[i])
        for i in range(count)
    ]
    zero = jnp.zeros((DK, DK), F32)
    state = jnp.concatenate([jnp.where(row == col, 1.0, 0.0), zero], axis=1)
    for i in range(count):
        from_state = dot(queries[i] - reads[i][:, :DK], state)
        emit(i, from_state[:, :DK], from_state[:, DK:] + reads[i][:, DK:])
        state = (
            state
            - dot(moves[i][:, :DK], state)
            + jnp.concatenate([zero, moves[i][:, DK:]], axis=1)
        )
    return state


def shard_kernel(x_ref, w_ref, beta_ref, state_ref, query_ref, own_ref, raw_ref):
    count = x_ref.shape[0] // CHUNK

    def project(i, carry):
        rows = pl.ds(pl.multiple_of(i * CHUNK, CHUNK), CHUNK)
        raw_ref[rows, :] = jnp.dot(x_ref[rows, :], w_ref[...], preferred_element_type=F32)
        return carry

    lax.fori_loop(0, count, project, 0)

    def emit(i, query, own):
        rows = pl.ds(i * CHUNK, CHUNK)
        query_ref[rows, :] = query.astype(BF16)
        own_ref[rows, :] = own

    raw = [
        [raw_ref[pl.ds(i * CHUNK, CHUNK), pl.ds(j * DK, DK)] for j in range(3)]
        for i in range(count)
    ]
    rates = [beta_ref[pl.ds(i * CHUNK, CHUNK), :] for i in range(count)]
    state_ref[...] = shard_maps(raw, rates, emit).astype(BF16)


def normed_kernel(shards, states_ref, query_ref, own_ref, gain_ref, out_ref):
    me = lax.axis_index("ctx")
    start = jnp.zeros((DK, DK), F32)
    for shard in range(shards - 1):
        state = states_ref[shard]
        after = dot(state[:, :DK], start) + state[:, DK:].astype(F32)
        start = jnp.where(shard < me, after, start)
    recurrent = own_ref[...] + dot(query_ref[...], start)
    scale = lax.rsqrt(jnp.mean(recurrent * recurrent, axis=-1, keepdims=True) + 1e-5)
    out_ref[...] = (recurrent * scale * gain_ref[...]).astype(BF16)


def local(tokens, beta, w_query, w_key, w_value, gain, w_out):
    rows = tokens.shape[0]
    shards, heads = lax.axis_size("ctx"), lax.axis_size("head")
    whole = pl.BlockSpec(memory_space=pltpu.VMEM)
    portion = lax.all_gather(tokens, "head", axis=1, tiled=True)
    weights = jnp.concatenate([w_query, w_key, w_value], axis=1)
    state, query, own = pl.pallas_call(
        shard_kernel,
        out_shape=(
            jax.ShapeDtypeStruct((DK, 2 * DK), BF16),
            jax.ShapeDtypeStruct((rows, DK), BF16),
            jax.ShapeDtypeStruct((rows, DK), F32),
        ),
        in_specs=[whole] * 3,
        out_specs=(whole,) * 3,
        scratch_shapes=[pltpu.VMEM((rows, 3 * DK), F32)],
        compiler_params=pltpu.CompilerParams(vmem_limit_bytes=40 * 2**20),
    )(portion, weights, beta)
    states = lax.all_gather(state, "ctx")
    normed = pl.pallas_call(
        functools.partial(normed_kernel, shards),
        out_shape=jax.ShapeDtypeStruct((rows, DK), BF16),
        in_specs=[whole] * 4,
        out_specs=whole,
        compiler_params=pltpu.CompilerParams(vmem_limit_bytes=20 * 2**20),
    )(states, query, own, gain.reshape(1, DK))
    parts = lax.all_to_all(normed.reshape(heads, rows // heads, DK), "head", 0, 0)
    w_all = lax.all_gather(w_out, "head", axis=0, tiled=True)
    mixed_rows = parts.transpose(1, 0, 2).reshape(rows // heads, heads * DK)
    return jnp.dot(mixed_rows, w_all, preferred_element_type=F32).astype(BF16)


def solution(mesh):
    placed = (
        P("ctx", "head"),
        P("ctx", "head"),
        P(None, "head"),
        P(None, "head"),
        P(None, "head"),
        P(),
        P("head", None),
    )
    return jax.shard_map(
        local, mesh=mesh, in_specs=placed, out_specs=P(("ctx", "head"), None), check_vma=False
    )
```

```python
import functools

import jax
import jax.numpy as jnp
from jax import lax
from jax.experimental import pallas as pl
from jax.experimental.pallas import tpu as pltpu
from jax.sharding import PartitionSpec as P

DK = 128
CHUNK = 128
F32, BF16 = jnp.float32, jnp.bfloat16


def dot(left, right):
    return jnp.dot(left.astype(BF16), right.astype(BF16), preferred_element_type=F32)


def dot_nt(left, right):
    return lax.dot_general(
        left.astype(BF16), right.astype(BF16), (((1,), (1,)), ((), ())), preferred_element_type=F32
    )


def dot_tn(left, right):
    return lax.dot_general(
        left.astype(BF16), right.astype(BF16), (((0,), (0,)), ((), ())), preferred_element_type=F32
    )


def unit_silu(raw):
    act = raw / (1.0 + jnp.exp(-raw))
    return act * lax.rsqrt(jnp.sum(act * act, axis=-1, keepdims=True) + 1e-6)


def unit_lower_inverses(lowers):
    size = lowers[0].shape[0]
    row = lax.broadcasted_iota(jnp.int32, (size, size), 0)
    col = lax.broadcasted_iota(jnp.int32, (size, size), 1)
    inverses = None
    level = 0
    while (1 << level) < size:
        mask = (
            ((row >> (level + 1)) == (col >> (level + 1)))
            & (((row >> level) & 1) == 1)
            & (((col >> level) & 1) == 0)
        )
        parts = [jnp.where(mask, lower, 0.0) for lower in lowers]
        if inverses is None:
            eye = jnp.where(row == col, 1.0, 0.0)
            inverses = [eye - part for part in parts]
        else:
            halves = [dot(inverse, part) for inverse, part in zip(inverses, parts)]
            inverses = [
                inverse - dot(half, inverse) for inverse, half in zip(inverses, halves)
            ]
        level += 1
    return inverses


def shard_maps(raw, rates, emit):
    count = len(raw)
    row = lax.broadcasted_iota(jnp.int32, (CHUNK, CHUNK), 0)
    col = lax.broadcasted_iota(jnp.int32, (CHUNK, CHUNK), 1)
    queries = [unit_silu(raw[i][0]) for i in range(count)]
    keys = [unit_silu(raw[i][1]) for i in range(count)]
    lowers = [
        jnp.where(row > col, rates[i] * dot_nt(keys[i], keys[i]), 0.0) for i in range(count)
    ]
    inverses = unit_lower_inverses(lowers)
    factors = [
        dot(inverses[i], jnp.concatenate([rates[i] * keys[i], rates[i] * raw[i][2]], axis=1))
        for i in range(count)
    ]
    moves = [dot_tn(keys[i], factors[i]) for i in range(count)]
    reads = [
        dot(jnp.where(row >= col, dot_nt(queries[i], keys[i]), 0.0), factors[i])
        for i in range(count)
    ]
    zero = jnp.zeros((DK, DK), F32)
    state = jnp.concatenate([jnp.where(row == col, 1.0, 0.0), zero], axis=1)
    for i in range(count):
        from_state = dot(queries[i] - reads[i][:, :DK], state)
        emit(i, from_state[:, :DK], from_state[:, DK:] + reads[i][:, DK:])
        state = (
            state
            - dot(moves[i][:, :DK], state)
            + jnp.concatenate([zero, moves[i][:, DK:]], axis=1)
        )
    return state


class LineGather:
    def __init__(self, own, slot, pieces, early, depth, width, sems, pending):
        self.own, self.slot, self.pieces, self.early = own, slot, pieces, early
        self.depth, self.width = depth, width
        self.recv, self.up, self.down, self.cross = sems
        self.pending = pending
        me = lax.axis_index("head")
        self.z, self.x = me // width, lax.rem(me, width)

    def head(self, z, j=0):
        return z * self.width + lax.rem(self.x + j, self.width)

    def send(self, cond, source, shard, piece, sem, target):
        def make():
            return pltpu.make_async_remote_copy(
                src_ref=source,
                dst_ref=self.slot(shard, piece),
                send_sem=sem,
                recv_sem=self.recv.at[shard, piece],
                device_id={"head": target},
                device_id_type=pl.DeviceIdType.MESH,
            )

        guarded(cond, lambda: make().start())
        self.pending.append((cond, make))

    def arrive(self, shard, piece):
        view = self.slot(shard, piece)
        pltpu.make_async_copy(view, view, self.recv.at[shard, piece]).wait()

    def send_up(self, source, shard, piece):
        self.send(
            self.z < self.depth - 1, source, shard, piece, self.up.at[shard, piece], self.head(self.z + 1)
        )

    def send_down(self, source, shard, piece):
        self.send(self.z > 0, source, shard, piece, self.down.at[shard, piece], self.head(self.z - 1))

    def send_across(self, cond, source, shard, piece):
        for j in range(1, self.width):
            self.send(
                cond, source, shard, piece, self.cross.at[j - 1, shard, piece], self.head(self.z, j)
            )

    def start(self):
        me = self.head(self.z)
        for piece in range(self.pieces):
            source = self.own(piece)
            self.send_across(None, source, me, piece)
            self.send_up(source, me, piece)
            self.send_down(source, me, piece)

    def start_early(self):
        for piece in range(self.early):
            for j in range(1, self.width):
                shard = self.head(self.z, j)
                self.arrive(shard, piece)
                self.send_up(self.slot(shard, piece), shard, piece)
                self.send_down(self.slot(shard, piece), shard, piece)

    def sides(self, distance):
        below, above = self.z - distance, self.z + distance
        return (
            (below >= 0, jnp.maximum(below, 0), True),
            (above < self.depth, jnp.minimum(above, self.depth - 1), False),
        )

    def stage(self, distance):
        for piece in range(self.pieces):
            for there, source_z, upward in self.sides(distance):
                for j in range(self.width if piece < self.early else 1):
                    shard = self.head(source_z, j)
                    view = self.slot(shard, piece)
                    guarded(there, functools.partial(self.arrive, shard, piece))
                    if upward and distance < self.depth - 1:
                        self.send(
                            there & (self.z < self.depth - 1), view, shard, piece,
                            self.up.at[shard, piece], self.head(self.z + 1),
                        )
                    elif distance < self.depth - 1:
                        self.send(
                            there & (self.z > 0), view, shard, piece,
                            self.down.at[shard, piece], self.head(self.z - 1),
                        )
                if piece >= self.early:
                    shard = self.head(source_z)
                    self.send_across(there, self.slot(shard, piece), shard, piece)

    def finish(self, shard):
        for piece in range(self.early, self.pieces):
            self.arrive(shard, piece)


def guarded(cond, action):
    if cond is None:
        action()
    else:
        pl.when(cond)(action)


TOKEN_PIECES, TOKEN_EARLY = 4, 1
OUT_PIECES, OUT_EARLY = 2, 0


def layer_kernel(
    shards, heads, depth,
    tokens_ref, beta_ref, wq_ref, wk_ref, wv_ref, gain_ref, wo_ref,
    out_ref,
    x_ref, w_ref, raw_ref, wo_all, query_ref, own_ref, states_ref, normed_ref, parts_ref,
    copy_sems, tok_recv, tok_up, tok_down, tok_cross,
    wo_recv, wo_up, wo_down, wo_cross, wo_swap_send, wo_swap_recv,
    state_send, state_recv, part_send, part_recv,
):
    ctx, head = lax.axis_index("ctx"), lax.axis_index("head")
    width = heads // depth
    rows, features = tokens_ref.shape
    core, partner = lax.rem(ctx, 2), ctx + 1 - 2 * lax.rem(ctx, 2)
    pending = []

    loads = [
        pltpu.make_async_copy(ref, w_ref.at[:, pl.ds(i * DK, DK)], copy_sems.at[i])
        for i, ref in enumerate((wq_ref, wk_ref, wv_ref))
    ]
    loads.append(pltpu.make_async_copy(tokens_ref, x_ref.at[head], copy_sems.at[3]))
    half = wo_ref.shape[0] // 2
    loads.append(pltpu.make_async_copy(wo_ref, wo_all.at[head], copy_sems.at[4]))
    for load in loads:
        load.start()

    barrier = pltpu.get_barrier_semaphore()
    for j in range(1, heads):
        pl.semaphore_signal(
            barrier, inc=1, device_id={"head": lax.rem(head + j, heads)},
            device_id_type=pl.DeviceIdType.MESH,
        )
    for j in range(1, shards):
        pl.semaphore_signal(
            barrier, inc=1, device_id={"ctx": lax.rem(ctx + j, shards)},
            device_id_type=pl.DeviceIdType.MESH,
        )
    pl.semaphore_wait(barrier, heads + shards - 2)

    piece_rows = rows // TOKEN_PIECES
    gather = LineGather(
        lambda piece: tokens_ref.at[pl.ds(piece * piece_rows, piece_rows)],
        lambda shard, piece: x_ref.at[shard, pl.ds(piece * piece_rows, piece_rows)],
        TOKEN_PIECES, TOKEN_EARLY, depth, width, (tok_recv, tok_up, tok_down, tok_cross), pending,
    )
    out_rows = half // OUT_PIECES

    def out_slot(shard, piece):
        start = pl.multiple_of(core * half + piece * out_rows, 16)
        return wo_all.at[shard, pl.ds(start, out_rows)]

    def out_own(piece):
        start = pl.multiple_of(core * half + piece * out_rows, 16)
        return wo_ref.at[pl.ds(start, out_rows)]

    spread = LineGather(
        out_own, out_slot, OUT_PIECES, OUT_EARLY, depth, width,
        (wo_recv, wo_up, wo_down, wo_cross), pending,
    )

    def swap(shard, cond):
        start = pl.multiple_of(core * half, 16)
        view = wo_all.at[shard, pl.ds(start, half)]

        def make():
            return pltpu.make_async_remote_copy(
                src_ref=view, dst_ref=view,
                send_sem=wo_swap_send.at[shard], recv_sem=wo_swap_recv.at[shard],
                device_id={"ctx": partner}, device_id_type=pl.DeviceIdType.MESH,
            )

        guarded(cond, lambda: make().start())
        pending.append((cond, make))

    def spread_stage(distance):
        if distance < depth:
            spread.stage(distance)
            for there, source_z, _ in spread.sides(distance):
                swap(spread.head(source_z), there)
        for index, (there, source_z, _) in enumerate(spread.sides(distance - 1)):
            if distance == 1 and index:
                continue
            for j in range(1, width):
                shard = spread.head(source_z, j)
                guarded(there, functools.partial(spread.finish, shard))
                swap(shard, there)

    def project(shard, first=False):
        tile = 256

        def step(i, carry):
            span = pl.ds(pl.multiple_of(i * tile, tile), tile)
            weight = w_ref[pl.ds(pl.multiple_of(shard * features, 128), features), :]
            term = jnp.dot(x_ref[shard, span, :], weight, preferred_element_type=F32)
            raw_ref[span, :] = term if first else raw_ref[span, :] + term
            return carry

        lax.fori_loop(0, rows // tile, step, 0)

    def finish_across(distance):
        for index, (there, source_z, _) in enumerate(gather.sides(distance)):
            if distance == 0 and index:
                continue
            for j in range(1, width):
                shard = gather.head(source_z, j)

                def take(shard=shard):
                    gather.finish(shard)
                    project(shard)

                guarded(there, take)

    gather.start()
    for load in loads[:4]:
        load.wait()
    gather.start_early()
    project(head, first=True)
    for distance in range(1, depth):
        gather.stage(distance)
        if distance == depth - 1:
            spread.start()
        for there, source_z, _ in gather.sides(distance):
            guarded(there, functools.partial(project, gather.head(source_z)))
        finish_across(distance - 1)
    finish_across(depth - 1)
    loads[4].wait()

    def emit(i, query, own):
        span = pl.ds(i * CHUNK, CHUNK)
        query_ref[span, :] = query.astype(BF16)
        own_ref[span, :] = own

    raw = [
        [raw_ref[pl.ds(i * CHUNK, CHUNK), pl.ds(j * DK, DK)] for j in range(3)]
        for i in range(rows // CHUNK)
    ]
    rates = [beta_ref[pl.ds(i * CHUNK, CHUNK), :] for i in range(rows // CHUNK)]
    states_ref[ctx] = shard_maps(raw, rates, emit).astype(BF16)

    for other in range(1, shards):
        def make(other=other):
            return pltpu.make_async_remote_copy(
                src_ref=states_ref.at[ctx], dst_ref=states_ref.at[ctx],
                send_sem=state_send.at[other], recv_sem=state_recv.at[ctx],
                device_id={"ctx": jnp.int32(other)}, device_id_type=pl.DeviceIdType.MESH,
            )

        guarded(ctx < other, lambda make=make: make().start())
        pending.append((ctx < other, make))

    spread_stage(1)
    for shard in range(shards - 1):
        @pl.when(shard < ctx)
        def _(shard=shard):
            view = states_ref.at[shard]
            pltpu.make_async_copy(view, view, state_recv.at[shard]).wait()

        @pl.when(shard >= ctx)
        def _(shard=shard):
            @pl.when(shard > ctx)
            def _():
                states_ref[shard] = jnp.zeros(states_ref.shape[1:], BF16)

    start = jnp.zeros((DK, DK), F32)
    for shard in range(shards - 1):
        state = states_ref[shard]
        after = dot(state[:, :DK], start) + state[:, DK:].astype(F32)
        start = jnp.where(shard < ctx, after, start)
    block = rows // heads
    for i in range(rows // CHUNK):
        span = pl.ds(i * CHUNK, CHUNK)
        recurrent = own_ref[span, :] + dot(query_ref[span, :], start)
        scale = lax.rsqrt(jnp.mean(recurrent * recurrent, axis=-1, keepdims=True) + 1e-5)
        normed_ref[span, :] = (recurrent * scale * gain_ref[...]).astype(BF16)

    mine = pl.multiple_of(head * DK, DK)
    own_part = pltpu.make_async_copy(
        normed_ref.at[pl.ds(pl.multiple_of(head * block, 16), block)],
        parts_ref.at[:, pl.ds(mine, DK)], copy_sems.at[5],
    )
    own_part.start()
    for j in range(1, heads):
        other = lax.rem(head + j, heads)

        def make(other=other, j=j):
            return pltpu.make_async_remote_copy(
                src_ref=normed_ref.at[pl.ds(pl.multiple_of(other * block, 16), block)],
                dst_ref=parts_ref.at[:, pl.ds(mine, DK)],
                send_sem=part_send.at[j], recv_sem=part_recv.at[j],
                device_id={"head": other}, device_id_type=pl.DeviceIdType.MESH,
            )

        make().start()
        pending.append((None, make))

    for distance in range(2, depth + 1):
        spread_stage(distance)
    for j in range(1, heads):
        source = lax.rem(head + heads - j, heads)
        view = parts_ref.at[:, pl.ds(pl.multiple_of(source * DK, DK), DK)]
        pltpu.make_async_copy(view, view, part_recv.at[j]).wait()
    own_part.wait()
    other_half = pl.multiple_of((1 - core) * half, 16)
    for j in range(1, heads):
        shard = lax.rem(head + j, heads)
        view = wo_all.at[shard, pl.ds(other_half, half)]
        pltpu.make_async_copy(view, view, wo_swap_recv.at[shard]).wait()

    tile = 512

    def mix(i, carry):
        span = pl.ds(pl.multiple_of(i * tile, tile), tile)
        weight = wo_all[:, :, span].reshape(heads * DK, tile)
        out_ref[:, span] = jnp.dot(parts_ref[...], weight, preferred_element_type=F32).astype(BF16)
        return carry

    lax.fori_loop(0, out_ref.shape[1] // tile, mix, 0)
    for cond, make in pending:
        guarded(cond, lambda make=make: make().wait_send())


def local(tokens, beta, w_query, w_key, w_value, gain, w_out):
    rows, features = tokens.shape
    shards, heads = lax.axis_size("ctx"), lax.axis_size("head")
    depth = 4 if heads % 4 == 0 else 1
    width = heads // depth
    model = w_query.shape[0]
    vmem, hbm = pl.BlockSpec(memory_space=pltpu.VMEM), pl.BlockSpec(memory_space=pl.ANY)
    dma = pltpu.SemaphoreType.DMA
    return pl.pallas_call(
        functools.partial(layer_kernel, shards, heads, depth),
        out_shape=jax.ShapeDtypeStruct((rows // heads, w_out.shape[1]), BF16),
        in_specs=[hbm, vmem, hbm, hbm, hbm, vmem, hbm],
        out_specs=vmem,
        scratch_shapes=[
            pltpu.VMEM((heads, rows, features), BF16),
            pltpu.VMEM((model, 3 * DK), BF16),
            pltpu.VMEM((rows, 3 * DK), F32),
            pltpu.VMEM((heads, DK, w_out.shape[1]), BF16),
            pltpu.VMEM((rows, DK), BF16),
            pltpu.VMEM((rows, DK), F32),
            pltpu.VMEM((shards, DK, 2 * DK), BF16),
            pltpu.VMEM((rows, DK), BF16),
            pltpu.VMEM((rows // heads, heads * DK), BF16),
            dma((6,)),
            dma((heads, TOKEN_PIECES)),
            dma((heads, TOKEN_PIECES)),
            dma((heads, TOKEN_PIECES)),
            dma((width - 1, heads, TOKEN_PIECES)),
            dma((heads, OUT_PIECES)),
            dma((heads, OUT_PIECES)),
            dma((heads, OUT_PIECES)),
            dma((width - 1, heads, OUT_PIECES)),
            dma((heads,)),
            dma((heads,)),
            dma((shards,)),
            dma((shards,)),
            dma((heads,)),
            dma((heads,)),
        ],
        compiler_params=pltpu.CompilerParams(
            collective_id=0, has_side_effects=True, vmem_limit_bytes=48 * 2**20
        ),
    )(tokens, beta, w_query, w_key, w_value, gain.reshape(1, DK), w_out)


def solution(mesh):
    placed = (
        P("ctx", "head"),
        P("ctx", "head"),
        P(None, "head"),
        P(None, "head"),
        P(None, "head"),
        P(),
        P("head", None),
    )
    return jax.shard_map(
        local, mesh=mesh, in_specs=placed, out_specs=P(("ctx", "head"), None), check_vma=False
    )
```

```python
import functools

import jax
import jax.numpy as jnp
from jax import lax
from jax.experimental import pallas as pl
from jax.experimental.pallas import tpu as pltpu
from jax.sharding import PartitionSpec as P

DK = 128
CHUNK = 128
F32, BF16 = jnp.float32, jnp.bfloat16


def dot(left, right):
    return jnp.dot(left.astype(BF16), right.astype(BF16), preferred_element_type=F32)


def dot_nt(left, right):
    return lax.dot_general(
        left.astype(BF16), right.astype(BF16), (((1,), (1,)), ((), ())), preferred_element_type=F32
    )


def dot_tn(left, right):
    return lax.dot_general(
        left.astype(BF16), right.astype(BF16), (((0,), (0,)), ((), ())), preferred_element_type=F32
    )


def unit_silu(raw):
    act = raw / (1.0 + jnp.exp(-raw))
    return act * lax.rsqrt(jnp.sum(act * act, axis=-1, keepdims=True) + 1e-6)


def unit_lower_inverses(lowers):
    size = lowers[0].shape[0]
    row = lax.broadcasted_iota(jnp.int32, (size, size), 0)
    col = lax.broadcasted_iota(jnp.int32, (size, size), 1)
    inverses = None
    level = 0
    while (1 << level) < size:
        mask = (
            ((row >> (level + 1)) == (col >> (level + 1)))
            & (((row >> level) & 1) == 1)
            & (((col >> level) & 1) == 0)
        )
        parts = [jnp.where(mask, lower, 0.0) for lower in lowers]
        if inverses is None:
            eye = jnp.where(row == col, 1.0, 0.0)
            inverses = [eye - part for part in parts]
        else:
            halves = [dot(inverse, part) for inverse, part in zip(inverses, parts)]
            inverses = [
                inverse - dot(half, inverse) for inverse, half in zip(inverses, halves)
            ]
        level += 1
    return inverses


def shard_maps(raw, rates, emit, midway):
    count = len(raw)
    row = lax.broadcasted_iota(jnp.int32, (CHUNK, CHUNK), 0)
    col = lax.broadcasted_iota(jnp.int32, (CHUNK, CHUNK), 1)
    queries = [unit_silu(raw[i][0]) for i in range(count)]
    keys = [unit_silu(raw[i][1]) for i in range(count)]
    lowers = [
        jnp.where(row > col, rates[i] * dot_nt(keys[i], keys[i]), 0.0) for i in range(count)
    ]
    inverses = unit_lower_inverses(lowers)
    midway()
    factors = [
        dot(inverses[i], jnp.concatenate([rates[i] * keys[i], rates[i] * raw[i][2]], axis=1))
        for i in range(count)
    ]
    moves = [dot_tn(keys[i], factors[i]) for i in range(count)]
    reads = [
        dot(jnp.where(row >= col, dot_nt(queries[i], keys[i]), 0.0), factors[i])
        for i in range(count)
    ]
    zero = jnp.zeros((DK, DK), F32)
    state = jnp.concatenate([jnp.where(row == col, 1.0, 0.0), zero], axis=1)
    for i in range(count):
        from_state = dot(queries[i] - reads[i][:, :DK], state)
        emit(i, from_state[:, :DK], from_state[:, DK:] + reads[i][:, DK:])
        state = (
            state
            - dot(moves[i][:, :DK], state)
            + jnp.concatenate([zero, moves[i][:, DK:]], axis=1)
        )
    return state


class LineGather:
    def __init__(self, own, slot, pieces, early, depth, width, sems, pending):
        self.own, self.slot, self.pieces, self.early = own, slot, pieces, early
        self.depth, self.width = depth, width
        self.recv, self.up, self.down, self.cross = sems
        self.pending = pending
        me = lax.axis_index("head")
        self.z, self.x = me // width, lax.rem(me, width)

    def head(self, z, j=0):
        return z * self.width + lax.rem(self.x + j, self.width)

    def send(self, cond, source, shard, piece, sem, target):
        def make():
            return pltpu.make_async_remote_copy(
                src_ref=source,
                dst_ref=self.slot(shard, piece),
                send_sem=sem,
                recv_sem=self.recv.at[shard, piece],
                device_id={"head": target},
                device_id_type=pl.DeviceIdType.MESH,
            )

        guarded(cond, lambda: make().start())
        self.pending.append((cond, make))

    def arrive(self, shard, piece):
        view = self.slot(shard, piece)
        pltpu.make_async_copy(view, view, self.recv.at[shard, piece]).wait()

    def send_up(self, source, shard, piece):
        self.send(
            self.z < self.depth - 1, source, shard, piece, self.up.at[shard, piece], self.head(self.z + 1)
        )

    def send_down(self, source, shard, piece):
        self.send(self.z > 0, source, shard, piece, self.down.at[shard, piece], self.head(self.z - 1))

    def send_across(self, cond, source, shard, piece):
        for j in range(1, self.width):
            self.send(
                cond, source, shard, piece, self.cross.at[j - 1, shard, piece], self.head(self.z, j)
            )

    def start(self):
        me = self.head(self.z)
        for piece in range(self.pieces):
            source = self.own(piece)
            self.send_across(None, source, me, piece)
            self.send_up(source, me, piece)
            self.send_down(source, me, piece)

    def start_early(self):
        for piece in range(self.early):
            for j in range(1, self.width):
                shard = self.head(self.z, j)
                self.arrive(shard, piece)
                self.send_up(self.slot(shard, piece), shard, piece)
                self.send_down(self.slot(shard, piece), shard, piece)

    def sides(self, distance):
        below, above = self.z - distance, self.z + distance
        return (
            (below >= 0, jnp.maximum(below, 0), True),
            (above < self.depth, jnp.minimum(above, self.depth - 1), False),
        )

    def stage(self, distance):
        for piece in range(self.pieces):
            for there, source_z, upward in self.sides(distance):
                for j in range(self.width if piece < self.early else 1):
                    shard = self.head(source_z, j)
                    view = self.slot(shard, piece)
                    guarded(there, functools.partial(self.arrive, shard, piece))
                    if upward and distance < self.depth - 1:
                        self.send(
                            there & (self.z < self.depth - 1), view, shard, piece,
                            self.up.at[shard, piece], self.head(self.z + 1),
                        )
                    elif distance < self.depth - 1:
                        self.send(
                            there & (self.z > 0), view, shard, piece,
                            self.down.at[shard, piece], self.head(self.z - 1),
                        )
                if piece >= self.early:
                    shard = self.head(source_z)
                    self.send_across(there, self.slot(shard, piece), shard, piece)

    def finish(self, shard):
        for piece in range(self.early, self.pieces):
            self.arrive(shard, piece)


def guarded(cond, action):
    if cond is None:
        action()
    else:
        pl.when(cond)(action)


TOKEN_PIECES, TOKEN_EARLY = 4, 1
OUT_PIECES, OUT_EARLY = 2, 0


def layer_kernel(
    shards, heads, depth,
    tokens_ref, beta_ref, wq_ref, wk_ref, wv_ref, gain_ref, wo_ref,
    out_ref,
    x_ref, w_ref, raw_ref, wo_all, query_ref, own_ref, states_ref, normed_ref, parts_ref,
    copy_sems, tok_recv, tok_up, tok_down, tok_cross,
    wo_recv, wo_up, wo_down, wo_cross, wo_swap_send, wo_swap_recv,
    state_send, state_recv, part_send, part_recv,
):
    ctx, head = lax.axis_index("ctx"), lax.axis_index("head")
    width = heads // depth
    rows, features = tokens_ref.shape
    core, partner = lax.rem(ctx, 2), ctx + 1 - 2 * lax.rem(ctx, 2)
    pending = []

    loads = [
        pltpu.make_async_copy(ref, w_ref.at[:, pl.ds(i * DK, DK)], copy_sems.at[i])
        for i, ref in enumerate((wq_ref, wk_ref, wv_ref))
    ]
    loads.append(pltpu.make_async_copy(tokens_ref, x_ref.at[head], copy_sems.at[3]))
    half = wo_ref.shape[0] // 2
    loads.append(pltpu.make_async_copy(wo_ref, wo_all.at[head], copy_sems.at[4]))
    for load in loads:
        load.start()

    barrier = pltpu.get_barrier_semaphore()
    for j in range(1, heads):
        pl.semaphore_signal(
            barrier, inc=1, device_id={"head": lax.rem(head + j, heads)},
            device_id_type=pl.DeviceIdType.MESH,
        )
    for j in range(1, shards):
        pl.semaphore_signal(
            barrier, inc=1, device_id={"ctx": lax.rem(ctx + j, shards)},
            device_id_type=pl.DeviceIdType.MESH,
        )
    pl.semaphore_wait(barrier, heads + shards - 2)

    piece_rows = rows // TOKEN_PIECES
    gather = LineGather(
        lambda piece: tokens_ref.at[pl.ds(piece * piece_rows, piece_rows)],
        lambda shard, piece: x_ref.at[shard, pl.ds(piece * piece_rows, piece_rows)],
        TOKEN_PIECES, TOKEN_EARLY, depth, width, (tok_recv, tok_up, tok_down, tok_cross), pending,
    )
    out_rows = half // OUT_PIECES

    def out_slot(shard, piece):
        start = pl.multiple_of(core * half + piece * out_rows, 16)
        return wo_all.at[shard, pl.ds(start, out_rows)]

    def out_own(piece):
        start = pl.multiple_of(core * half + piece * out_rows, 16)
        return wo_ref.at[pl.ds(start, out_rows)]

    spread = LineGather(
        out_own, out_slot, OUT_PIECES, OUT_EARLY, depth, width,
        (wo_recv, wo_up, wo_down, wo_cross), pending,
    )

    def swap(shard, cond):
        start = pl.multiple_of(core * half, 16)
        view = wo_all.at[shard, pl.ds(start, half)]

        def make():
            return pltpu.make_async_remote_copy(
                src_ref=view, dst_ref=view,
                send_sem=wo_swap_send.at[shard], recv_sem=wo_swap_recv.at[shard],
                device_id={"ctx": partner}, device_id_type=pl.DeviceIdType.MESH,
            )

        guarded(cond, lambda: make().start())
        pending.append((cond, make))

    def spread_stage(distance):
        spread.stage(distance)
        for there, source_z, _ in spread.sides(distance):
            swap(spread.head(source_z), there)

    def spread_across(distance):
        for index, (there, source_z, _) in enumerate(spread.sides(distance)):
            if distance == 0 and index:
                continue
            for j in range(1, width):
                shard = spread.head(source_z, j)
                guarded(there, functools.partial(spread.finish, shard))
                swap(shard, there)

    def project(shard, first=False):
        tile = 256

        def step(i, carry):
            span = pl.ds(pl.multiple_of(i * tile, tile), tile)
            weight = w_ref[pl.ds(pl.multiple_of(shard * features, 128), features), :]
            term = jnp.dot(x_ref[shard, span, :], weight, preferred_element_type=F32)
            raw_ref[span, :] = term if first else raw_ref[span, :] + term
            return carry

        lax.fori_loop(0, rows // tile, step, 0)

    def finish_across(distance):
        for index, (there, source_z, _) in enumerate(gather.sides(distance)):
            if distance == 0 and index:
                continue
            for j in range(1, width):
                shard = gather.head(source_z, j)

                def take(shard=shard):
                    gather.finish(shard)
                    project(shard)

                guarded(there, take)

    gather.start()
    for load in loads[:4]:
        load.wait()
    gather.start_early()
    project(head, first=True)
    for distance in range(1, depth):
        gather.stage(distance)
        if distance == 1:
            spread.start()
        if distance == depth - 1:
            spread_stage(1)
        for there, source_z, _ in gather.sides(distance):
            guarded(there, functools.partial(project, gather.head(source_z)))
        finish_across(distance - 1)
    finish_across(depth - 1)
    loads[4].wait()

    def emit(i, query, own):
        span = pl.ds(i * CHUNK, CHUNK)
        query_ref[span, :] = query.astype(BF16)
        own_ref[span, :] = own

    raw = [
        [raw_ref[pl.ds(i * CHUNK, CHUNK), pl.ds(j * DK, DK)] for j in range(3)]
        for i in range(rows // CHUNK)
    ]
    rate_columns = beta_ref[...].T
    rates = [rate_columns[:, i : i + 1] for i in range(rows // CHUNK)]
    states_ref[ctx] = shard_maps(raw, rates, emit, functools.partial(spread_stage, 2)).astype(BF16)

    for other in range(1, shards):
        def make(other=other):
            return pltpu.make_async_remote_copy(
                src_ref=states_ref.at[ctx], dst_ref=states_ref.at[ctx],
                send_sem=state_send.at[other], recv_sem=state_recv.at[ctx],
                device_id={"ctx": jnp.int32(other)}, device_id_type=pl.DeviceIdType.MESH,
            )

        guarded(ctx < other, lambda make=make: make().start())
        pending.append((ctx < other, make))

    spread_stage(3)
    for shard in range(shards - 1):
        @pl.when(shard < ctx)
        def _(shard=shard):
            view = states_ref.at[shard]
            pltpu.make_async_copy(view, view, state_recv.at[shard]).wait()

        @pl.when(shard >= ctx)
        def _(shard=shard):
            @pl.when(shard > ctx)
            def _():
                states_ref[shard] = jnp.zeros(states_ref.shape[1:], BF16)

    start = jnp.zeros((DK, DK), F32)
    for shard in range(shards - 1):
        state = states_ref[shard]
        after = dot(state[:, :DK], start) + state[:, DK:].astype(F32)
        start = jnp.where(shard < ctx, after, start)
    block = rows // heads
    for i in range(rows // CHUNK):
        span = pl.ds(i * CHUNK, CHUNK)
        recurrent = own_ref[span, :] + dot(query_ref[span, :], start)
        scale = lax.rsqrt(jnp.mean(recurrent * recurrent, axis=-1, keepdims=True) + 1e-5)
        normed_ref[span, :] = (recurrent * scale * gain_ref[...]).astype(BF16)

    mine = pl.multiple_of(head * DK, DK)
    own_part = pltpu.make_async_copy(
        normed_ref.at[pl.ds(pl.multiple_of(head * block, 16), block)],
        parts_ref.at[:, pl.ds(mine, DK)], copy_sems.at[5],
    )
    own_part.start()
    for j in range(1, heads):
        other = lax.rem(head + j, heads)

        def make(other=other, j=j):
            return pltpu.make_async_remote_copy(
                src_ref=normed_ref.at[pl.ds(pl.multiple_of(other * block, 16), block)],
                dst_ref=parts_ref.at[:, pl.ds(mine, DK)],
                send_sem=part_send.at[j], recv_sem=part_recv.at[j],
                device_id={"head": other}, device_id_type=pl.DeviceIdType.MESH,
            )

        make().start()
        pending.append((None, make))

    for distance in range(depth):
        spread_across(distance)
    for j in range(1, heads):
        source = lax.rem(head + heads - j, heads)
        view = parts_ref.at[:, pl.ds(pl.multiple_of(source * DK, DK), DK)]
        pltpu.make_async_copy(view, view, part_recv.at[j]).wait()
    own_part.wait()
    other_half = pl.multiple_of((1 - core) * half, 16)
    for j in range(1, heads):
        shard = lax.rem(head + j, heads)
        view = wo_all.at[shard, pl.ds(other_half, half)]
        pltpu.make_async_copy(view, view, wo_swap_recv.at[shard]).wait()

    tile = 512

    def mix(i, carry):
        span = pl.ds(pl.multiple_of(i * tile, tile), tile)
        weight = wo_all[:, :, span].reshape(heads * DK, tile)
        out_ref[:, span] = jnp.dot(parts_ref[...], weight, preferred_element_type=F32).astype(BF16)
        return carry

    lax.fori_loop(0, out_ref.shape[1] // tile, mix, 0)
    for cond, make in pending:
        guarded(cond, lambda make=make: make().wait_send())


def local(tokens, beta, w_query, w_key, w_value, gain, w_out):
    rows, features = tokens.shape
    shards, heads = lax.axis_size("ctx"), lax.axis_size("head")
    depth = 4
    width = heads // depth
    model = w_query.shape[0]
    vmem, hbm = pl.BlockSpec(memory_space=pltpu.VMEM), pl.BlockSpec(memory_space=pl.ANY)
    dma = pltpu.SemaphoreType.DMA
    return pl.pallas_call(
        functools.partial(layer_kernel, shards, heads, depth),
        out_shape=jax.ShapeDtypeStruct((rows // heads, w_out.shape[1]), BF16),
        in_specs=[hbm, vmem, hbm, hbm, hbm, vmem, hbm],
        out_specs=vmem,
        scratch_shapes=[
            pltpu.VMEM((heads, rows, features), BF16),
            pltpu.VMEM((model, 3 * DK), BF16),
            pltpu.VMEM((rows, 3 * DK), F32),
            pltpu.VMEM((heads, DK, w_out.shape[1]), BF16),
            pltpu.VMEM((rows, DK), BF16),
            pltpu.VMEM((rows, DK), F32),
            pltpu.VMEM((shards, DK, 2 * DK), BF16),
            pltpu.VMEM((rows, DK), BF16),
            pltpu.VMEM((rows // heads, heads * DK), BF16),
            dma((6,)),
            dma((heads, TOKEN_PIECES)),
            dma((heads, TOKEN_PIECES)),
            dma((heads, TOKEN_PIECES)),
            dma((width - 1, heads, TOKEN_PIECES)),
            dma((heads, OUT_PIECES)),
            dma((heads, OUT_PIECES)),
            dma((heads, OUT_PIECES)),
            dma((width - 1, heads, OUT_PIECES)),
            dma((heads,)),
            dma((heads,)),
            dma((shards,)),
            dma((shards,)),
            dma((heads,)),
            dma((heads,)),
        ],
        compiler_params=pltpu.CompilerParams(
            collective_id=0, has_side_effects=True, vmem_limit_bytes=60 * 2**20
        ),
    )(tokens, beta.reshape(rows // CHUNK, CHUNK), w_query, w_key, w_value, gain.reshape(1, DK), w_out)


def solution(mesh):
    placed = (
        P("ctx", "head"),
        P("ctx", "head"),
        P(None, "head"),
        P(None, "head"),
        P(None, "head"),
        P(),
        P("head", None),
    )
    return jax.shard_map(
        local, mesh=mesh, in_specs=placed, out_specs=P(("ctx", "head"), None), check_vma=False
    )
```

```python
import functools

import jax
import jax.numpy as jnp
from jax import lax
from jax.experimental import pallas as pl
from jax.experimental.pallas import tpu as pltpu
from jax.sharding import PartitionSpec as P

DK = 128
CHUNK = 128
F32, BF16 = jnp.float32, jnp.bfloat16


def dot(left, right):
    return jnp.dot(left.astype(BF16), right.astype(BF16), preferred_element_type=F32)


def dot_nt(left, right):
    return lax.dot_general(
        left.astype(BF16), right.astype(BF16), (((1,), (1,)), ((), ())), preferred_element_type=F32
    )


def dot_tn(left, right):
    return lax.dot_general(
        left.astype(BF16), right.astype(BF16), (((0,), (0,)), ((), ())), preferred_element_type=F32
    )


def unit_silu(raw):
    act = raw / (1.0 + jnp.exp(-raw))
    return act * lax.rsqrt(jnp.sum(act * act, axis=-1, keepdims=True) + 1e-6)


def unit_lower_inverses(lowers):
    size = lowers[0].shape[0]
    row = lax.broadcasted_iota(jnp.int32, (size, size), 0)
    col = lax.broadcasted_iota(jnp.int32, (size, size), 1)
    inverses = None
    level = 0
    while (1 << level) < size:
        mask = (
            ((row >> (level + 1)) == (col >> (level + 1)))
            & (((row >> level) & 1) == 1)
            & (((col >> level) & 1) == 0)
        )
        parts = [jnp.where(mask, lower, 0.0) for lower in lowers]
        if inverses is None:
            eye = jnp.where(row == col, 1.0, 0.0)
            inverses = [eye - part for part in parts]
        else:
            halves = [dot(inverse, part) for inverse, part in zip(inverses, parts)]
            inverses = [
                inverse - dot(half, inverse) for inverse, half in zip(inverses, halves)
            ]
        level += 1
    return inverses


def shard_maps(raw, rates, emit, midway):
    count = len(raw)
    row = lax.broadcasted_iota(jnp.int32, (CHUNK, CHUNK), 0)
    col = lax.broadcasted_iota(jnp.int32, (CHUNK, CHUNK), 1)
    queries = [unit_silu(raw[i][0]) for i in range(count)]
    keys = [unit_silu(raw[i][1]) for i in range(count)]
    lowers = [
        jnp.where(row > col, rates[i] * dot_nt(keys[i], keys[i]), 0.0) for i in range(count)
    ]
    inverses = unit_lower_inverses(lowers)
    midway()
    factors = [
        dot(inverses[i], jnp.concatenate([rates[i] * keys[i], rates[i] * raw[i][2]], axis=1))
        for i in range(count)
    ]
    moves = [dot_tn(keys[i], factors[i]) for i in range(count)]
    reads = [
        dot(jnp.where(row >= col, dot_nt(queries[i], keys[i]), 0.0), factors[i])
        for i in range(count)
    ]
    zero = jnp.zeros((DK, DK), F32)
    state = jnp.concatenate([jnp.where(row == col, 1.0, 0.0), zero], axis=1)
    for i in range(count):
        from_state = dot(queries[i] - reads[i][:, :DK], state)
        emit(i, from_state[:, :DK], from_state[:, DK:] + reads[i][:, DK:])
        state = (
            state
            - dot(moves[i][:, :DK], state)
            + jnp.concatenate([zero, moves[i][:, DK:]], axis=1)
        )
    return state


class LineGather:
    def __init__(self, own, slot, pieces, early, depth, width, sems, pending):
        self.own, self.slot, self.pieces, self.early = own, slot, pieces, early
        self.depth, self.width = depth, width
        self.recv, self.up, self.down, self.cross = sems
        self.pending = pending
        me = lax.axis_index("head")
        self.z, self.x = me // width, lax.rem(me, width)

    def head(self, z, j=0):
        return z * self.width + lax.rem(self.x + j, self.width)

    def send(self, cond, source, shard, piece, sem, target):
        def make():
            return pltpu.make_async_remote_copy(
                src_ref=source,
                dst_ref=self.slot(shard, piece),
                send_sem=sem,
                recv_sem=self.recv.at[shard, piece],
                device_id={"head": target},
                device_id_type=pl.DeviceIdType.MESH,
            )

        guarded(cond, lambda: make().start())
        self.pending.append((cond, make))

    def arrive(self, shard, piece):
        view = self.slot(shard, piece)
        pltpu.make_async_copy(view, view, self.recv.at[shard, piece]).wait()

    def send_up(self, source, shard, piece):
        self.send(
            self.z < self.depth - 1, source, shard, piece, self.up.at[shard, piece], self.head(self.z + 1)
        )

    def send_down(self, source, shard, piece):
        self.send(self.z > 0, source, shard, piece, self.down.at[shard, piece], self.head(self.z - 1))

    def send_across(self, cond, source, shard, piece):
        for j in range(1, self.width):
            self.send(
                cond, source, shard, piece, self.cross.at[j - 1, shard, piece], self.head(self.z, j)
            )

    def start(self):
        me = self.head(self.z)
        for piece in range(self.pieces):
            source = self.own(piece)
            self.send_across(None, source, me, piece)
            self.send_up(source, me, piece)
            self.send_down(source, me, piece)

    def start_early(self):
        for piece in range(self.early):
            for j in range(1, self.width):
                shard = self.head(self.z, j)
                self.arrive(shard, piece)
                self.send_up(self.slot(shard, piece), shard, piece)
                self.send_down(self.slot(shard, piece), shard, piece)

    def sides(self, distance):
        below, above = self.z - distance, self.z + distance
        return (
            (below >= 0, jnp.maximum(below, 0), True),
            (above < self.depth, jnp.minimum(above, self.depth - 1), False),
        )

    def stage(self, distance):
        for piece in range(self.pieces):
            for there, source_z, upward in self.sides(distance):
                for j in range(self.width if piece < self.early else 1):
                    shard = self.head(source_z, j)
                    view = self.slot(shard, piece)
                    guarded(there, functools.partial(self.arrive, shard, piece))
                    if upward and distance < self.depth - 1:
                        self.send(
                            there & (self.z < self.depth - 1), view, shard, piece,
                            self.up.at[shard, piece], self.head(self.z + 1),
                        )
                    elif distance < self.depth - 1:
                        self.send(
                            there & (self.z > 0), view, shard, piece,
                            self.down.at[shard, piece], self.head(self.z - 1),
                        )
                if piece >= self.early:
                    shard = self.head(source_z)
                    self.send_across(there, self.slot(shard, piece), shard, piece)

    def finish(self, shard):
        for piece in range(self.early, self.pieces):
            self.arrive(shard, piece)


def guarded(cond, action):
    if cond is None:
        action()
    else:
        pl.when(cond)(action)


TOKEN_PIECES, TOKEN_EARLY = 4, 1
OUT_PIECES, OUT_EARLY = 1, 0


def layer_kernel(
    shards, heads, depth,
    tokens_ref, beta_ref, wq_ref, wk_ref, wv_ref, gain_ref, wo_ref,
    out_ref,
    x_ref, w_ref, raw_ref, wo_all, query_ref, own_ref, states_ref, normed_ref, parts_ref,
    copy_sems, tok_recv, tok_up, tok_down, tok_cross,
    wo_recv, wo_up, wo_down, wo_cross, core_send, core_recv, pair_send, pair_recv,
    state_send, state_recv, part_send, part_recv,
):
    ctx, head = lax.axis_index("ctx"), lax.axis_index("head")
    width = heads // depth
    rows, features = tokens_ref.shape
    core, pair = lax.rem(ctx, 2), lax.rem(ctx // 2, 2)
    core_partner, pair_partner = ctx + 1 - 2 * core, ctx + 2 - 4 * pair
    pending = []

    loads = [
        pltpu.make_async_copy(ref, w_ref.at[:, pl.ds(i * DK, DK)], copy_sems.at[i])
        for i, ref in enumerate((wq_ref, wk_ref, wv_ref))
    ]
    loads.append(pltpu.make_async_copy(tokens_ref, x_ref.at[head], copy_sems.at[3]))
    quarter = wo_ref.shape[0] // 4
    loads.append(pltpu.make_async_copy(wo_ref, wo_all.at[head], copy_sems.at[4]))
    for load in loads:
        load.start()

    barrier = pltpu.get_barrier_semaphore()
    for j in range(1, heads):
        pl.semaphore_signal(
            barrier, inc=1, device_id={"head": lax.rem(head + j, heads)},
            device_id_type=pl.DeviceIdType.MESH,
        )
    for j in range(1, shards):
        pl.semaphore_signal(
            barrier, inc=1, device_id={"ctx": lax.rem(ctx + j, shards)},
            device_id_type=pl.DeviceIdType.MESH,
        )
    pl.semaphore_wait(barrier, heads + shards - 2)

    piece_rows = rows // TOKEN_PIECES
    gather = LineGather(
        lambda piece: tokens_ref.at[pl.ds(piece * piece_rows, piece_rows)],
        lambda shard, piece: x_ref.at[shard, pl.ds(piece * piece_rows, piece_rows)],
        TOKEN_PIECES, TOKEN_EARLY, depth, width, (tok_recv, tok_up, tok_down, tok_cross), pending,
    )
    out_rows = quarter // OUT_PIECES

    def quarter_start(pair, core):
        return (2 * pair + core) * quarter

    def out_slot(shard, piece):
        start = pl.multiple_of(quarter_start(pair, core) + piece * out_rows, 16)
        return wo_all.at[shard, pl.ds(start, out_rows)]

    def out_own(piece):
        start = pl.multiple_of(quarter_start(pair, core) + piece * out_rows, 16)
        return wo_ref.at[pl.ds(start, out_rows)]

    def out_quarter(shard, pair, core):
        return wo_all.at[shard, pl.ds(pl.multiple_of(quarter_start(pair, core), 16), quarter)]

    spread = LineGather(
        out_own, out_slot, OUT_PIECES, OUT_EARLY, depth, width,
        (wo_recv, wo_up, wo_down, wo_cross), pending,
    )

    def hand_over(cond, view, send_sem, recv_sem, target):
        def make():
            return pltpu.make_async_remote_copy(
                src_ref=view, dst_ref=view, send_sem=send_sem, recv_sem=recv_sem,
                device_id={"ctx": target}, device_id_type=pl.DeviceIdType.MESH,
            )

        guarded(cond, lambda: make().start())
        pending.append((cond, make))

    def swap(shard, cond):
        view = out_quarter(shard, pair, core)
        hand_over(cond, view, pair_send.at[shard], pair_recv.at[shard], pair_partner)
        hand_over(cond, view, core_send.at[shard, 0], core_recv.at[shard, 0], core_partner)

    def swap_paired(shard, cond):
        view = out_quarter(shard, 1 - pair, core)
        guarded(cond, pltpu.make_async_copy(view, view, pair_recv.at[shard]).wait)
        hand_over(cond, view, core_send.at[shard, 1], core_recv.at[shard, 1], core_partner)

    def spread_stage(distance):
        spread.stage(distance)
        for there, source_z, _ in spread.sides(distance):
            swap(spread.head(source_z), there)

    def spread_across(distance):
        for index, (there, source_z, _) in enumerate(spread.sides(distance)):
            if distance == 0 and index:
                continue
            for j in range(1, width):
                shard = spread.head(source_z, j)
                guarded(there, functools.partial(spread.finish, shard))
                swap(shard, there)

    def project(shard, first=False):
        tile = 256

        def step(i, carry):
            span = pl.ds(pl.multiple_of(i * tile, tile), tile)
            weight = w_ref[pl.ds(pl.multiple_of(shard * features, 128), features), :]
            term = jnp.dot(x_ref[shard, span, :], weight, preferred_element_type=F32)
            raw_ref[span, :] = term if first else raw_ref[span, :] + term
            return carry

        lax.fori_loop(0, rows // tile, step, 0)

    def finish_across(distance):
        for index, (there, source_z, _) in enumerate(gather.sides(distance)):
            if distance == 0 and index:
                continue
            for j in range(1, width):
                shard = gather.head(source_z, j)

                def take(shard=shard):
                    gather.finish(shard)
                    project(shard)

                guarded(there, take)

    gather.start()
    for load in loads[:4]:
        load.wait()
    gather.start_early()
    project(head, first=True)
    for distance in range(1, depth):
        gather.stage(distance)
        if distance == 2:
            spread.start()
        for there, source_z, _ in gather.sides(distance):
            guarded(there, functools.partial(project, gather.head(source_z)))
        finish_across(distance - 1)
    spread_stage(1)
    finish_across(depth - 1)
    loads[4].wait()

    def midway():
        spread_across(0)
        spread_stage(2)

    def emit(i, query, own):
        span = pl.ds(i * CHUNK, CHUNK)
        query_ref[span, :] = query.astype(BF16)
        own_ref[span, :] = own

    raw = [
        [raw_ref[pl.ds(i * CHUNK, CHUNK), pl.ds(j * DK, DK)] for j in range(3)]
        for i in range(rows // CHUNK)
    ]
    rate_columns = beta_ref[...].T
    rates = [rate_columns[:, i : i + 1] for i in range(rows // CHUNK)]
    states_ref[ctx] = shard_maps(raw, rates, emit, midway).astype(BF16)

    for other in range(1, shards):
        def make(other=other):
            return pltpu.make_async_remote_copy(
                src_ref=states_ref.at[ctx], dst_ref=states_ref.at[ctx],
                send_sem=state_send.at[other], recv_sem=state_recv.at[ctx],
                device_id={"ctx": jnp.int32(other)}, device_id_type=pl.DeviceIdType.MESH,
            )

        guarded(ctx < other, lambda make=make: make().start())
        pending.append((ctx < other, make))

    spread_stage(3)
    for shard in range(shards - 1):
        @pl.when(shard < ctx)
        def _(shard=shard):
            view = states_ref.at[shard]
            pltpu.make_async_copy(view, view, state_recv.at[shard]).wait()

        @pl.when(shard >= ctx)
        def _(shard=shard):
            @pl.when(shard > ctx)
            def _():
                states_ref[shard] = jnp.zeros(states_ref.shape[1:], BF16)

    start = jnp.zeros((DK, DK), F32)
    for shard in range(shards - 1):
        state = states_ref[shard]
        after = dot(state[:, :DK], start) + state[:, DK:].astype(F32)
        start = jnp.where(shard < ctx, after, start)
    block = rows // heads
    for i in range(rows // CHUNK):
        span = pl.ds(i * CHUNK, CHUNK)
        recurrent = own_ref[span, :] + dot(query_ref[span, :], start)
        scale = lax.rsqrt(jnp.mean(recurrent * recurrent, axis=-1, keepdims=True) + 1e-5)
        normed_ref[span, :] = (recurrent * scale * gain_ref[...]).astype(BF16)

    mine = pl.multiple_of(head * DK, DK)
    own_part = pltpu.make_async_copy(
        normed_ref.at[pl.ds(pl.multiple_of(head * block, 16), block)],
        parts_ref.at[:, pl.ds(mine, DK)], copy_sems.at[5],
    )
    own_part.start()
    for j in range(1, heads):
        other = lax.rem(head + j, heads)

        def make(other=other, j=j):
            return pltpu.make_async_remote_copy(
                src_ref=normed_ref.at[pl.ds(pl.multiple_of(other * block, 16), block)],
                dst_ref=parts_ref.at[:, pl.ds(mine, DK)],
                send_sem=part_send.at[j], recv_sem=part_recv.at[j],
                device_id={"head": other}, device_id_type=pl.DeviceIdType.MESH,
            )

        make().start()
        pending.append((None, make))

    for distance in range(1, depth):
        spread_across(distance)
    for distance in range(depth):
        for index, (there, source_z, _) in enumerate(spread.sides(distance)):
            if distance == 0 and index:
                continue
            for j in range(0 if distance else 1, width):
                swap_paired(spread.head(source_z, j), there)
    for j in range(1, heads):
        source = lax.rem(head + heads - j, heads)
        view = parts_ref.at[:, pl.ds(pl.multiple_of(source * DK, DK), DK)]
        pltpu.make_async_copy(view, view, part_recv.at[j]).wait()
    own_part.wait()
    for j in range(1, heads):
        shard = lax.rem(head + j, heads)
        for index, from_pair in enumerate((pair, 1 - pair)):
            view = out_quarter(shard, from_pair, 1 - core)
            pltpu.make_async_copy(view, view, core_recv.at[shard, index]).wait()

    tile = 512

    def mix(i, carry):
        span = pl.ds(pl.multiple_of(i * tile, tile), tile)
        weight = wo_all[:, :, span].reshape(heads * DK, tile)
        out_ref[:, span] = jnp.dot(parts_ref[...], weight, preferred_element_type=F32).astype(BF16)
        return carry

    lax.fori_loop(0, out_ref.shape[1] // tile, mix, 0)
    for cond, make in pending:
        guarded(cond, lambda make=make: make().wait_send())


def local(tokens, beta, w_query, w_key, w_value, gain, w_out):
    rows, features = tokens.shape
    shards, heads = lax.axis_size("ctx"), lax.axis_size("head")
    depth = 4
    width = heads // depth
    model = w_query.shape[0]
    vmem, hbm = pl.BlockSpec(memory_space=pltpu.VMEM), pl.BlockSpec(memory_space=pl.ANY)
    dma = pltpu.SemaphoreType.DMA
    return pl.pallas_call(
        functools.partial(layer_kernel, shards, heads, depth),
        out_shape=jax.ShapeDtypeStruct((rows // heads, w_out.shape[1]), BF16),
        in_specs=[hbm, vmem, hbm, hbm, hbm, vmem, hbm],
        out_specs=vmem,
        scratch_shapes=[
            pltpu.VMEM((heads, rows, features), BF16),
            pltpu.VMEM((model, 3 * DK), BF16),
            pltpu.VMEM((rows, 3 * DK), F32),
            pltpu.VMEM((heads, DK, w_out.shape[1]), BF16),
            pltpu.VMEM((rows, DK), BF16),
            pltpu.VMEM((rows, DK), F32),
            pltpu.VMEM((shards, DK, 2 * DK), BF16),
            pltpu.VMEM((rows, DK), BF16),
            pltpu.VMEM((rows // heads, heads * DK), BF16),
            dma((6,)),
            dma((heads, TOKEN_PIECES)),
            dma((heads, TOKEN_PIECES)),
            dma((heads, TOKEN_PIECES)),
            dma((width - 1, heads, TOKEN_PIECES)),
            dma((heads, OUT_PIECES)),
            dma((heads, OUT_PIECES)),
            dma((heads, OUT_PIECES)),
            dma((width - 1, heads, OUT_PIECES)),
            dma((heads, 2)),
            dma((heads, 2)),
            dma((heads,)),
            dma((heads,)),
            dma((shards,)),
            dma((shards,)),
            dma((heads,)),
            dma((heads,)),
        ],
        compiler_params=pltpu.CompilerParams(
            collective_id=0, has_side_effects=True, vmem_limit_bytes=60 * 2**20
        ),
    )(tokens, beta.reshape(rows // CHUNK, CHUNK), w_query, w_key, w_value, gain.reshape(1, DK), w_out)


def solution(mesh):
    placed = (
        P("ctx", "head"),
        P("ctx", "head"),
        P(None, "head"),
        P(None, "head"),
        P(None, "head"),
        P(),
        P("head", None),
    )
    return jax.shard_map(
        local, mesh=mesh, in_specs=placed, out_specs=P(("ctx", "head"), None), check_vma=False
    )
```

```python
import functools

import jax
import jax.numpy as jnp
from jax import lax
from jax.experimental import pallas as pl
from jax.experimental.pallas import tpu as pltpu
from jax.sharding import PartitionSpec as P

DK = 128
CHUNK = 128
F32, BF16 = jnp.float32, jnp.bfloat16


def dot(left, right):
    return jnp.dot(left.astype(BF16), right.astype(BF16), preferred_element_type=F32)


def dot_nt(left, right):
    return lax.dot_general(
        left.astype(BF16), right.astype(BF16), (((1,), (1,)), ((), ())), preferred_element_type=F32
    )


def dot_tn(left, right):
    return lax.dot_general(
        left.astype(BF16), right.astype(BF16), (((0,), (0,)), ((), ())), preferred_element_type=F32
    )


def unit_silu(raw):
    act = raw / (1.0 + jnp.exp(-raw))
    return act * lax.rsqrt(jnp.sum(act * act, axis=-1, keepdims=True) + 1e-6)


def unit_lower_inverses(lowers):
    size = lowers[0].shape[0]
    row = lax.broadcasted_iota(jnp.int32, (size, size), 0)
    col = lax.broadcasted_iota(jnp.int32, (size, size), 1)
    inverses = None
    level = 0
    while (1 << level) < size:
        mask = (
            ((row >> (level + 1)) == (col >> (level + 1)))
            & (((row >> level) & 1) == 1)
            & (((col >> level) & 1) == 0)
        )
        parts = [jnp.where(mask, lower, 0.0) for lower in lowers]
        if inverses is None:
            eye = jnp.where(row == col, 1.0, 0.0)
            inverses = [eye - part for part in parts]
        else:
            halves = [dot(inverse, part) for inverse, part in zip(inverses, parts)]
            inverses = [
                inverse - dot(half, inverse) for inverse, half in zip(inverses, halves)
            ]
        level += 1
    return inverses


def shard_maps(raw, rates, emit, midway):
    count = len(raw)
    row = lax.broadcasted_iota(jnp.int32, (CHUNK, CHUNK), 0)
    col = lax.broadcasted_iota(jnp.int32, (CHUNK, CHUNK), 1)
    queries = [unit_silu(raw[i][0]) for i in range(count)]
    keys = [unit_silu(raw[i][1]) for i in range(count)]
    lowers = [
        jnp.where(row > col, rates[i] * dot_nt(keys[i], keys[i]), 0.0) for i in range(count)
    ]
    inverses = unit_lower_inverses(lowers)
    midway()
    factors = [
        dot(inverses[i], jnp.concatenate([rates[i] * keys[i], rates[i] * raw[i][2]], axis=1))
        for i in range(count)
    ]
    moves = [dot_tn(keys[i], factors[i]) for i in range(count)]
    reads = [
        dot(jnp.where(row >= col, dot_nt(queries[i], keys[i]), 0.0), factors[i])
        for i in range(count)
    ]
    zero = jnp.zeros((DK, DK), F32)
    state = jnp.concatenate([jnp.where(row == col, 1.0, 0.0), zero], axis=1)
    for i in range(count):
        from_state = dot(queries[i] - reads[i][:, :DK], state)
        emit(i, from_state[:, :DK], from_state[:, DK:] + reads[i][:, DK:])
        state = (
            state
            - dot(moves[i][:, :DK], state)
            + jnp.concatenate([zero, moves[i][:, DK:]], axis=1)
        )
    return state


class LineGather:
    def __init__(self, own, slot, pieces, early, depth, width, sems, pending):
        self.own, self.slot, self.pieces, self.early = own, slot, pieces, early
        self.depth, self.width = depth, width
        self.recv, self.up, self.down, self.cross = sems
        self.pending = pending
        me = lax.axis_index("head")
        self.z, self.x = me // width, lax.rem(me, width)

    def head(self, z, j=0):
        return z * self.width + lax.rem(self.x + j, self.width)

    def send(self, cond, source, shard, piece, sem, target):
        def make():
            return pltpu.make_async_remote_copy(
                src_ref=source,
                dst_ref=self.slot(shard, piece),
                send_sem=sem,
                recv_sem=self.recv.at[shard, piece],
                device_id={"head": target},
                device_id_type=pl.DeviceIdType.MESH,
            )

        guarded(cond, lambda: make().start())
        self.pending.append((cond, make))

    def arrive(self, shard, piece):
        view = self.slot(shard, piece)
        pltpu.make_async_copy(view, view, self.recv.at[shard, piece]).wait()

    def send_up(self, source, shard, piece):
        self.send(
            self.z < self.depth - 1, source, shard, piece, self.up.at[shard, piece], self.head(self.z + 1)
        )

    def send_down(self, source, shard, piece):
        self.send(self.z > 0, source, shard, piece, self.down.at[shard, piece], self.head(self.z - 1))

    def send_across(self, cond, source, shard, piece):
        for j in range(1, self.width):
            self.send(
                cond, source, shard, piece, self.cross.at[j - 1, shard, piece], self.head(self.z, j)
            )

    def start(self):
        me = self.head(self.z)
        for piece in range(self.pieces):
            source = self.own(piece)
            self.send_across(None, source, me, piece)
            self.send_up(source, me, piece)
            self.send_down(source, me, piece)

    def start_early(self):
        for piece in range(self.early):
            for j in range(1, self.width):
                shard = self.head(self.z, j)
                self.arrive(shard, piece)
                self.send_up(self.slot(shard, piece), shard, piece)
                self.send_down(self.slot(shard, piece), shard, piece)

    def sides(self, distance):
        below, above = self.z - distance, self.z + distance
        return (
            (below >= 0, jnp.maximum(below, 0), True),
            (above < self.depth, jnp.minimum(above, self.depth - 1), False),
        )

    def stage(self, distance):
        for piece in range(self.pieces):
            for there, source_z, upward in self.sides(distance):
                for j in range(self.width if piece < self.early else 1):
                    shard = self.head(source_z, j)
                    view = self.slot(shard, piece)
                    guarded(there, functools.partial(self.arrive, shard, piece))
                    if upward and distance < self.depth - 1:
                        self.send(
                            there & (self.z < self.depth - 1), view, shard, piece,
                            self.up.at[shard, piece], self.head(self.z + 1),
                        )
                    elif distance < self.depth - 1:
                        self.send(
                            there & (self.z > 0), view, shard, piece,
                            self.down.at[shard, piece], self.head(self.z - 1),
                        )
                if piece >= self.early:
                    shard = self.head(source_z)
                    self.send_across(there, self.slot(shard, piece), shard, piece)

    def finish(self, shard):
        for piece in range(self.early, self.pieces):
            self.arrive(shard, piece)


def guarded(cond, action):
    if cond is None:
        action()
    else:
        pl.when(cond)(action)


TOKEN_PIECES, TOKEN_EARLY = 4, 0
OUT_PIECES, OUT_EARLY = 1, 0


def layer_kernel(
    shards, heads, depth,
    tokens_ref, beta_ref, wq_ref, wk_ref, wv_ref, gain_ref, wo_ref,
    out_ref,
    x_ref, w_ref, raw_ref, wo_all, query_ref, own_ref, states_ref, normed_ref, parts_ref,
    copy_sems, tok_recv, tok_up, tok_down, tok_cross,
    wo_recv, wo_up, wo_down, wo_cross, core_send, core_recv, pair_send, pair_recv,
    state_send, state_recv, part_send, part_recv,
):
    ctx, head = lax.axis_index("ctx"), lax.axis_index("head")
    width = heads // depth
    rows, features = tokens_ref.shape
    core, pair = lax.rem(ctx, 2), lax.rem(ctx // 2, 2)
    core_partner, pair_partner = ctx + 1 - 2 * core, ctx + 2 - 4 * pair
    pending = []

    loads = [
        pltpu.make_async_copy(ref, w_ref.at[:, pl.ds(i * DK, DK)], copy_sems.at[i])
        for i, ref in enumerate((wq_ref, wk_ref, wv_ref))
    ]
    loads.append(pltpu.make_async_copy(tokens_ref, x_ref.at[head], copy_sems.at[3]))
    quarter = wo_ref.shape[0] // 4
    loads.append(pltpu.make_async_copy(wo_ref, wo_all.at[head], copy_sems.at[4]))
    for load in loads:
        load.start()

    barrier = pltpu.get_barrier_semaphore()
    for j in range(1, heads):
        pl.semaphore_signal(
            barrier, inc=1, device_id={"head": lax.rem(head + j, heads)},
            device_id_type=pl.DeviceIdType.MESH,
        )
    for j in range(1, shards):
        pl.semaphore_signal(
            barrier, inc=1, device_id={"ctx": lax.rem(ctx + j, shards)},
            device_id_type=pl.DeviceIdType.MESH,
        )
    pl.semaphore_wait(barrier, heads + shards - 2)

    piece_rows = rows // TOKEN_PIECES
    gather = LineGather(
        lambda piece: tokens_ref.at[pl.ds(piece * piece_rows, piece_rows)],
        lambda shard, piece: x_ref.at[shard, pl.ds(piece * piece_rows, piece_rows)],
        TOKEN_PIECES, TOKEN_EARLY, depth, width, (tok_recv, tok_up, tok_down, tok_cross), pending,
    )
    out_rows = quarter // OUT_PIECES

    def quarter_start(pair, core):
        return (2 * pair + core) * quarter

    def out_slot(shard, piece):
        start = pl.multiple_of(quarter_start(pair, core) + piece * out_rows, 16)
        return wo_all.at[shard, pl.ds(start, out_rows)]

    def out_own(piece):
        start = pl.multiple_of(quarter_start(pair, core) + piece * out_rows, 16)
        return wo_ref.at[pl.ds(start, out_rows)]

    def out_quarter(shard, pair, core):
        return wo_all.at[shard, pl.ds(pl.multiple_of(quarter_start(pair, core), 16), quarter)]

    spread = LineGather(
        out_own, out_slot, OUT_PIECES, OUT_EARLY, depth, width,
        (wo_recv, wo_up, wo_down, wo_cross), pending,
    )

    def hand_over(cond, view, send_sem, recv_sem, target):
        def make():
            return pltpu.make_async_remote_copy(
                src_ref=view, dst_ref=view, send_sem=send_sem, recv_sem=recv_sem,
                device_id={"ctx": target}, device_id_type=pl.DeviceIdType.MESH,
            )

        guarded(cond, lambda: make().start())
        pending.append((cond, make))

    def swap(shard, cond):
        view = out_quarter(shard, pair, core)
        hand_over(cond, view, pair_send.at[shard], pair_recv.at[shard], pair_partner)
        hand_over(cond, view, core_send.at[shard, 0], core_recv.at[shard, 0], core_partner)

    def swap_paired(shard, cond):
        view = out_quarter(shard, 1 - pair, core)
        guarded(cond, pltpu.make_async_copy(view, view, pair_recv.at[shard]).wait)
        hand_over(cond, view, core_send.at[shard, 1], core_recv.at[shard, 1], core_partner)

    def spread_stage(distance):
        spread.stage(distance)
        for there, source_z, _ in spread.sides(distance):
            swap(spread.head(source_z), there)

    def spread_across(distance):
        for index, (there, source_z, _) in enumerate(spread.sides(distance)):
            if distance == 0 and index:
                continue
            for j in range(1, width):
                shard = spread.head(source_z, j)
                guarded(there, functools.partial(spread.finish, shard))
                swap(shard, there)

    def project(shard, first=False):
        tile = 256

        def step(i, carry):
            span = pl.ds(pl.multiple_of(i * tile, tile), tile)
            weight = w_ref[pl.ds(pl.multiple_of(shard * features, 128), features), :]
            term = jnp.dot(x_ref[shard, span, :], weight, preferred_element_type=F32)
            raw_ref[span, :] = term if first else raw_ref[span, :] + term
            return carry

        lax.fori_loop(0, rows // tile, step, 0)

    def finish_across(distance):
        for index, (there, source_z, _) in enumerate(gather.sides(distance)):
            if distance == 0 and index:
                continue
            for j in range(1, width):
                shard = gather.head(source_z, j)

                def take(shard=shard):
                    gather.finish(shard)
                    project(shard)

                guarded(there, take)

    gather.start()
    for load in loads[:4]:
        load.wait()
    gather.start_early()
    project(head, first=True)
    for distance in range(1, depth):
        gather.stage(distance)
        if distance == 2:
            spread.start()
        for there, source_z, _ in gather.sides(distance):
            guarded(there, functools.partial(project, gather.head(source_z)))
        finish_across(distance - 1)
    spread_stage(1)
    finish_across(depth - 1)
    loads[4].wait()

    def midway():
        spread_across(0)
        spread_stage(2)

    def emit(i, query, own):
        span = pl.ds(i * CHUNK, CHUNK)
        query_ref[span, :] = query.astype(BF16)
        own_ref[span, :] = own

    raw = [
        [raw_ref[pl.ds(i * CHUNK, CHUNK), pl.ds(j * DK, DK)] for j in range(3)]
        for i in range(rows // CHUNK)
    ]
    rate_columns = beta_ref[...].T
    rates = [rate_columns[:, i : i + 1] for i in range(rows // CHUNK)]
    states_ref[ctx] = shard_maps(raw, rates, emit, midway).astype(BF16)

    for other in range(1, shards):
        def make(other=other):
            return pltpu.make_async_remote_copy(
                src_ref=states_ref.at[ctx], dst_ref=states_ref.at[ctx],
                send_sem=state_send.at[other], recv_sem=state_recv.at[ctx],
                device_id={"ctx": jnp.int32(other)}, device_id_type=pl.DeviceIdType.MESH,
            )

        guarded(ctx < other, lambda make=make: make().start())
        pending.append((ctx < other, make))

    spread_stage(3)
    for shard in range(shards - 1):
        @pl.when(shard < ctx)
        def _(shard=shard):
            view = states_ref.at[shard]
            pltpu.make_async_copy(view, view, state_recv.at[shard]).wait()

        @pl.when(shard >= ctx)
        def _(shard=shard):
            @pl.when(shard > ctx)
            def _():
                states_ref[shard] = jnp.zeros(states_ref.shape[1:], BF16)

    start = jnp.zeros((DK, DK), F32)
    for shard in range(shards - 1):
        state = states_ref[shard]
        after = dot(state[:, :DK], start) + state[:, DK:].astype(F32)
        start = jnp.where(shard < ctx, after, start)
    block = rows // heads
    for i in range(rows // CHUNK):
        span = pl.ds(i * CHUNK, CHUNK)
        recurrent = own_ref[span, :] + dot(query_ref[span, :], start)
        scale = lax.rsqrt(jnp.mean(recurrent * recurrent, axis=-1, keepdims=True) + 1e-5)
        normed_ref[span, :] = (recurrent * scale * gain_ref[...]).astype(BF16)

    mine = pl.multiple_of(head * DK, DK)
    own_part = pltpu.make_async_copy(
        normed_ref.at[pl.ds(pl.multiple_of(head * block, 16), block)],
        parts_ref.at[:, pl.ds(mine, DK)], copy_sems.at[5],
    )
    own_part.start()
    for j in range(1, heads):
        other = lax.rem(head + j, heads)

        def make(other=other, j=j):
            return pltpu.make_async_remote_copy(
                src_ref=normed_ref.at[pl.ds(pl.multiple_of(other * block, 16), block)],
                dst_ref=parts_ref.at[:, pl.ds(mine, DK)],
                send_sem=part_send.at[j], recv_sem=part_recv.at[j],
                device_id={"head": other}, device_id_type=pl.DeviceIdType.MESH,
            )

        make().start()
        pending.append((None, make))

    for distance in range(1, depth):
        spread_across(distance)
    for distance in range(depth):
        for index, (there, source_z, _) in enumerate(spread.sides(distance)):
            if distance == 0 and index:
                continue
            for j in range(0 if distance else 1, width):
                swap_paired(spread.head(source_z, j), there)
    for j in range(1, heads):
        source = lax.rem(head + heads - j, heads)
        view = parts_ref.at[:, pl.ds(pl.multiple_of(source * DK, DK), DK)]
        pltpu.make_async_copy(view, view, part_recv.at[j]).wait()
    own_part.wait()
    for j in range(1, heads):
        shard = lax.rem(head + j, heads)
        for index, from_pair in enumerate((pair, 1 - pair)):
            view = out_quarter(shard, from_pair, 1 - core)
            pltpu.make_async_copy(view, view, core_recv.at[shard, index]).wait()

    tile = 512

    def mix(i, carry):
        span = pl.ds(pl.multiple_of(i * tile, tile), tile)
        weight = wo_all[:, :, span].reshape(heads * DK, tile)
        out_ref[:, span] = jnp.dot(parts_ref[...], weight, preferred_element_type=F32).astype(BF16)
        return carry

    lax.fori_loop(0, out_ref.shape[1] // tile, mix, 0)
    for cond, make in pending:
        guarded(cond, lambda make=make: make().wait_send())


def local(tokens, beta, w_query, w_key, w_value, gain, w_out):
    rows, features = tokens.shape
    shards, heads = lax.axis_size("ctx"), lax.axis_size("head")
    depth = 4
    width = heads // depth
    model = w_query.shape[0]
    vmem, hbm = pl.BlockSpec(memory_space=pltpu.VMEM), pl.BlockSpec(memory_space=pl.ANY)
    dma = pltpu.SemaphoreType.DMA
    return pl.pallas_call(
        functools.partial(layer_kernel, shards, heads, depth),
        out_shape=jax.ShapeDtypeStruct((rows // heads, w_out.shape[1]), BF16),
        in_specs=[hbm, vmem, hbm, hbm, hbm, vmem, hbm],
        out_specs=vmem,
        scratch_shapes=[
            pltpu.VMEM((heads, rows, features), BF16),
            pltpu.VMEM((model, 3 * DK), BF16),
            pltpu.VMEM((rows, 3 * DK), F32),
            pltpu.VMEM((heads, DK, w_out.shape[1]), BF16),
            pltpu.VMEM((rows, DK), BF16),
            pltpu.VMEM((rows, DK), F32),
            pltpu.VMEM((shards, DK, 2 * DK), BF16),
            pltpu.VMEM((rows, DK), BF16),
            pltpu.VMEM((rows // heads, heads * DK), BF16),
            dma((6,)),
            dma((heads, TOKEN_PIECES)),
            dma((heads, TOKEN_PIECES)),
            dma((heads, TOKEN_PIECES)),
            dma((width - 1, heads, TOKEN_PIECES)),
            dma((heads, OUT_PIECES)),
            dma((heads, OUT_PIECES)),
            dma((heads, OUT_PIECES)),
            dma((width - 1, heads, OUT_PIECES)),
            dma((heads, 2)),
            dma((heads, 2)),
            dma((heads,)),
            dma((heads,)),
            dma((shards,)),
            dma((shards,)),
            dma((heads,)),
            dma((heads,)),
        ],
        compiler_params=pltpu.CompilerParams(
            collective_id=0, has_side_effects=True, vmem_limit_bytes=60 * 2**20
        ),
    )(tokens, beta.reshape(rows // CHUNK, CHUNK), w_query, w_key, w_value, gain.reshape(1, DK), w_out)


def solution(mesh):
    placed = (
        P("ctx", "head"),
        P("ctx", "head"),
        P(None, "head"),
        P(None, "head"),
        P(None, "head"),
        P(),
        P("head", None),
    )
    return jax.shard_map(
        local, mesh=mesh, in_specs=placed, out_specs=P(("ctx", "head"), None), check_vma=False
    )
```

```python
import functools

import jax
import jax.numpy as jnp
from jax import lax
from jax.experimental import pallas as pl
from jax.experimental.pallas import tpu as pltpu
from jax.sharding import PartitionSpec as P

DK = 128
CHUNK = 128
F32, BF16 = jnp.float32, jnp.bfloat16


def dot(left, right):
    return jnp.dot(left.astype(BF16), right.astype(BF16), preferred_element_type=F32)


def dot_nt(left, right):
    return lax.dot_general(
        left.astype(BF16), right.astype(BF16), (((1,), (1,)), ((), ())), preferred_element_type=F32
    )


def dot_tn(left, right):
    return lax.dot_general(
        left.astype(BF16), right.astype(BF16), (((0,), (0,)), ((), ())), preferred_element_type=F32
    )


def unit_silu(raw):
    act = raw / (1.0 + jnp.exp(-raw))
    return act * lax.rsqrt(jnp.sum(act * act, axis=-1, keepdims=True) + 1e-6)


def unit_lower_inverses(lowers):
    size = lowers[0].shape[0]
    row = lax.broadcasted_iota(jnp.int32, (size, size), 0)
    col = lax.broadcasted_iota(jnp.int32, (size, size), 1)
    inverses = None
    level = 0
    while (1 << level) < size:
        mask = (
            ((row >> (level + 1)) == (col >> (level + 1)))
            & (((row >> level) & 1) == 1)
            & (((col >> level) & 1) == 0)
        )
        parts = [jnp.where(mask, lower, 0.0) for lower in lowers]
        if inverses is None:
            eye = jnp.where(row == col, 1.0, 0.0)
            inverses = [eye - part for part in parts]
        else:
            halves = [dot(inverse, part) for inverse, part in zip(inverses, parts)]
            inverses = [
                inverse - dot(half, inverse) for inverse, half in zip(inverses, halves)
            ]
        level += 1
    return inverses


def shard_maps(raw, rates, emit, midway):
    count = len(raw)
    row = lax.broadcasted_iota(jnp.int32, (CHUNK, CHUNK), 0)
    col = lax.broadcasted_iota(jnp.int32, (CHUNK, CHUNK), 1)
    queries = [unit_silu(raw[i][0]) for i in range(count)]
    keys = [unit_silu(raw[i][1]) for i in range(count)]
    lowers = [
        jnp.where(row > col, rates[i] * dot_nt(keys[i], keys[i]), 0.0) for i in range(count)
    ]
    inverses = unit_lower_inverses(lowers)
    midway()
    factors = [
        dot(inverses[i], jnp.concatenate([rates[i] * keys[i], rates[i] * raw[i][2]], axis=1))
        for i in range(count)
    ]
    moves = [dot_tn(keys[i], factors[i]) for i in range(count)]
    reads = [
        dot(jnp.where(row >= col, dot_nt(queries[i], keys[i]), 0.0), factors[i])
        for i in range(count)
    ]
    zero = jnp.zeros((DK, DK), F32)
    state = jnp.concatenate([jnp.where(row == col, 1.0, 0.0), zero], axis=1)
    for i in range(count):
        from_state = dot(queries[i] - reads[i][:, :DK], state)
        emit(i, from_state[:, :DK], from_state[:, DK:] + reads[i][:, DK:])
        state = (
            state
            - dot(moves[i][:, :DK], state)
            + jnp.concatenate([zero, moves[i][:, DK:]], axis=1)
        )
    return state


class LineGather:
    def __init__(self, own, slot, pieces, early, depth, width, sems, pending):
        self.own, self.slot, self.pieces, self.early = own, slot, pieces, early
        self.depth, self.width = depth, width
        self.recv, self.up, self.down, self.cross = sems
        self.pending = pending
        me = lax.axis_index("head")
        self.z, self.x = me // width, lax.rem(me, width)

    def head(self, z, j=0):
        return z * self.width + lax.rem(self.x + j, self.width)

    def send(self, cond, source, shard, piece, sem, target):
        def make():
            return pltpu.make_async_remote_copy(
                src_ref=source,
                dst_ref=self.slot(shard, piece),
                send_sem=sem,
                recv_sem=self.recv.at[shard, piece],
                device_id={"head": target},
                device_id_type=pl.DeviceIdType.MESH,
            )

        guarded(cond, lambda: make().start())
        self.pending.append((cond, make))

    def arrive(self, shard, piece):
        view = self.slot(shard, piece)
        pltpu.make_async_copy(view, view, self.recv.at[shard, piece]).wait()

    def send_up(self, source, shard, piece):
        self.send(
            self.z < self.depth - 1, source, shard, piece, self.up.at[shard, piece], self.head(self.z + 1)
        )

    def send_down(self, source, shard, piece):
        self.send(self.z > 0, source, shard, piece, self.down.at[shard, piece], self.head(self.z - 1))

    def send_across(self, cond, source, shard, piece):
        for j in range(1, self.width):
            self.send(
                cond, source, shard, piece, self.cross.at[j - 1, shard, piece], self.head(self.z, j)
            )

    def start(self):
        me = self.head(self.z)
        for piece in range(self.pieces):
            source = self.own(piece)
            self.send_across(None, source, me, piece)
            self.send_up(source, me, piece)
            self.send_down(source, me, piece)

    def start_early(self):
        for piece in range(self.early):
            for j in range(1, self.width):
                shard = self.head(self.z, j)
                self.arrive(shard, piece)
                self.send_up(self.slot(shard, piece), shard, piece)
                self.send_down(self.slot(shard, piece), shard, piece)

    def sides(self, distance):
        below, above = self.z - distance, self.z + distance
        return (
            (below >= 0, jnp.maximum(below, 0), True),
            (above < self.depth, jnp.minimum(above, self.depth - 1), False),
        )

    def stage(self, distance):
        for piece in range(self.pieces):
            for there, source_z, upward in self.sides(distance):
                for j in range(self.width if piece < self.early else 1):
                    shard = self.head(source_z, j)
                    view = self.slot(shard, piece)
                    guarded(there, functools.partial(self.arrive, shard, piece))
                    if upward and distance < self.depth - 1:
                        self.send(
                            there & (self.z < self.depth - 1), view, shard, piece,
                            self.up.at[shard, piece], self.head(self.z + 1),
                        )
                    elif distance < self.depth - 1:
                        self.send(
                            there & (self.z > 0), view, shard, piece,
                            self.down.at[shard, piece], self.head(self.z - 1),
                        )
                if piece >= self.early:
                    shard = self.head(source_z)
                    self.send_across(there, self.slot(shard, piece), shard, piece)

    def finish(self, shard):
        for piece in range(self.early, self.pieces):
            self.arrive(shard, piece)


def guarded(cond, action):
    if cond is None:
        action()
    else:
        pl.when(cond)(action)


TOKEN_PIECES, TOKEN_EARLY = 4, 0
OUT_PIECES, OUT_EARLY = 1, 1


def layer_kernel(
    shards, heads, depth,
    tokens_ref, beta_ref, wq_ref, wk_ref, wv_ref, gain_ref, wo_ref,
    out_ref,
    x_ref, w_ref, raw_ref, wo_all, query_ref, own_ref, states_ref, normed_ref, parts_ref,
    copy_sems, tok_recv, tok_up, tok_down, tok_cross,
    wo_recv, wo_up, wo_down, wo_cross, core_send, core_recv, pair_send, pair_recv,
    state_send, state_recv, part_send, part_recv,
):
    ctx, head = lax.axis_index("ctx"), lax.axis_index("head")
    width = heads // depth
    rows, features = tokens_ref.shape
    core, pair = lax.rem(ctx, 2), lax.rem(ctx // 2, 2)
    core_partner, pair_partner = ctx + 1 - 2 * core, ctx + 2 - 4 * pair
    pending = []

    loads = [
        pltpu.make_async_copy(ref, w_ref.at[:, pl.ds(i * DK, DK)], copy_sems.at[i])
        for i, ref in enumerate((wq_ref, wk_ref, wv_ref))
    ]
    loads.append(pltpu.make_async_copy(tokens_ref, x_ref.at[head], copy_sems.at[3]))
    quarter = wo_ref.shape[0] // 4
    loads.append(pltpu.make_async_copy(wo_ref, wo_all.at[head], copy_sems.at[4]))
    for load in loads:
        load.start()

    barrier = pltpu.get_barrier_semaphore()
    for j in range(1, heads):
        pl.semaphore_signal(
            barrier, inc=1, device_id={"head": lax.rem(head + j, heads)},
            device_id_type=pl.DeviceIdType.MESH,
        )
    for j in range(1, shards):
        pl.semaphore_signal(
            barrier, inc=1, device_id={"ctx": lax.rem(ctx + j, shards)},
            device_id_type=pl.DeviceIdType.MESH,
        )
    pl.semaphore_wait(barrier, heads + shards - 2)

    piece_rows = rows // TOKEN_PIECES
    gather = LineGather(
        lambda piece: tokens_ref.at[pl.ds(piece * piece_rows, piece_rows)],
        lambda shard, piece: x_ref.at[shard, pl.ds(piece * piece_rows, piece_rows)],
        TOKEN_PIECES, TOKEN_EARLY, depth, width, (tok_recv, tok_up, tok_down, tok_cross), pending,
    )
    out_rows = quarter // OUT_PIECES

    def quarter_start(pair, core):
        return (2 * pair + core) * quarter

    def out_slot(shard, piece):
        start = pl.multiple_of(quarter_start(pair, core) + piece * out_rows, 16)
        return wo_all.at[shard, pl.ds(start, out_rows)]

    def out_own(piece):
        start = pl.multiple_of(quarter_start(pair, core) + piece * out_rows, 16)
        return wo_ref.at[pl.ds(start, out_rows)]

    def out_quarter(shard, pair, core):
        return wo_all.at[shard, pl.ds(pl.multiple_of(quarter_start(pair, core), 16), quarter)]

    spread = LineGather(
        out_own, out_slot, OUT_PIECES, OUT_EARLY, depth, width,
        (wo_recv, wo_up, wo_down, wo_cross), pending,
    )

    def hand_over(cond, view, send_sem, recv_sem, target):
        def make():
            return pltpu.make_async_remote_copy(
                src_ref=view, dst_ref=view, send_sem=send_sem, recv_sem=recv_sem,
                device_id={"ctx": target}, device_id_type=pl.DeviceIdType.MESH,
            )

        guarded(cond, lambda: make().start())
        pending.append((cond, make))

    def swap(shard, cond):
        view = out_quarter(shard, pair, core)
        hand_over(cond, view, pair_send.at[shard], pair_recv.at[shard], pair_partner)
        hand_over(cond, view, core_send.at[shard, 0], core_recv.at[shard, 0], core_partner)

    def swap_paired(shard, cond):
        view = out_quarter(shard, 1 - pair, core)
        guarded(cond, pltpu.make_async_copy(view, view, pair_recv.at[shard]).wait)
        hand_over(cond, view, core_send.at[shard, 1], core_recv.at[shard, 1], core_partner)

    def at_distance(distance, action):
        for index, (there, source_z, _) in enumerate(spread.sides(distance)):
            if distance == 0 and index:
                continue
            for j in range(0 if distance else 1, width):
                action(spread.head(source_z, j), there)

    def project(shard, first=False):
        tile = 256

        def step(i, carry):
            span = pl.ds(pl.multiple_of(i * tile, tile), tile)
            weight = w_ref[pl.ds(pl.multiple_of(shard * features, 128), features), :]
            term = jnp.dot(x_ref[shard, span, :], weight, preferred_element_type=F32)
            raw_ref[span, :] = term if first else raw_ref[span, :] + term
            return carry

        lax.fori_loop(0, rows // tile, step, 0)

    def finish_across(distance):
        for index, (there, source_z, _) in enumerate(gather.sides(distance)):
            if distance == 0 and index:
                continue
            for j in range(1, width):
                shard = gather.head(source_z, j)

                def take(shard=shard):
                    gather.finish(shard)
                    project(shard)

                guarded(there, take)

    spread.start()
    gather.start()
    for load in loads[:4]:
        load.wait()
    spread.start_early()
    at_distance(0, swap)
    gather.start_early()
    project(head, first=True)
    for distance in range(1, depth):
        gather.stage(distance)
        spread.stage(distance)
        at_distance(distance, swap)
        at_distance(distance - 1, swap_paired)
        for there, source_z, _ in gather.sides(distance):
            guarded(there, functools.partial(project, gather.head(source_z)))
        finish_across(distance - 1)
    finish_across(depth - 1)
    loads[4].wait()

    def midway():
        at_distance(depth - 1, swap_paired)

    def emit(i, query, own):
        span = pl.ds(i * CHUNK, CHUNK)
        query_ref[span, :] = query.astype(BF16)
        own_ref[span, :] = own

    raw = [
        [raw_ref[pl.ds(i * CHUNK, CHUNK), pl.ds(j * DK, DK)] for j in range(3)]
        for i in range(rows // CHUNK)
    ]
    rate_columns = beta_ref[...].T
    rates = [rate_columns[:, i : i + 1] for i in range(rows // CHUNK)]
    states_ref[ctx] = shard_maps(raw, rates, emit, midway).astype(BF16)

    for other in range(1, shards):
        def make(other=other):
            return pltpu.make_async_remote_copy(
                src_ref=states_ref.at[ctx], dst_ref=states_ref.at[ctx],
                send_sem=state_send.at[other], recv_sem=state_recv.at[ctx],
                device_id={"ctx": jnp.int32(other)}, device_id_type=pl.DeviceIdType.MESH,
            )

        guarded(ctx < other, lambda make=make: make().start())
        pending.append((ctx < other, make))

    for shard in range(shards - 1):
        @pl.when(shard < ctx)
        def _(shard=shard):
            view = states_ref.at[shard]
            pltpu.make_async_copy(view, view, state_recv.at[shard]).wait()

        @pl.when(shard >= ctx)
        def _(shard=shard):
            @pl.when(shard > ctx)
            def _():
                states_ref[shard] = jnp.zeros(states_ref.shape[1:], BF16)

    start = jnp.zeros((DK, DK), F32)
    for shard in range(shards - 1):
        state = states_ref[shard]
        after = dot(state[:, :DK], start) + state[:, DK:].astype(F32)
        start = jnp.where(shard < ctx, after, start)
    block = rows // heads
    for i in range(rows // CHUNK):
        span = pl.ds(i * CHUNK, CHUNK)
        recurrent = own_ref[span, :] + dot(query_ref[span, :], start)
        scale = lax.rsqrt(jnp.mean(recurrent * recurrent, axis=-1, keepdims=True) + 1e-5)
        normed_ref[span, :] = (recurrent * scale * gain_ref[...]).astype(BF16)

    mine = pl.multiple_of(head * DK, DK)
    own_part = pltpu.make_async_copy(
        normed_ref.at[pl.ds(pl.multiple_of(head * block, 16), block)],
        parts_ref.at[:, pl.ds(mine, DK)], copy_sems.at[5],
    )
    own_part.start()
    for j in range(1, heads):
        other = lax.rem(head + j, heads)

        def make(other=other, j=j):
            return pltpu.make_async_remote_copy(
                src_ref=normed_ref.at[pl.ds(pl.multiple_of(other * block, 16), block)],
                dst_ref=parts_ref.at[:, pl.ds(mine, DK)],
                send_sem=part_send.at[j], recv_sem=part_recv.at[j],
                device_id={"head": other}, device_id_type=pl.DeviceIdType.MESH,
            )

        make().start()
        pending.append((None, make))

    for j in range(1, heads):
        source = lax.rem(head + heads - j, heads)
        view = parts_ref.at[:, pl.ds(pl.multiple_of(source * DK, DK), DK)]
        pltpu.make_async_copy(view, view, part_recv.at[j]).wait()
    own_part.wait()
    for j in range(1, heads):
        shard = lax.rem(head + j, heads)
        for index, from_pair in enumerate((pair, 1 - pair)):
            view = out_quarter(shard, from_pair, 1 - core)
            pltpu.make_async_copy(view, view, core_recv.at[shard, index]).wait()

    tile = 512

    def mix(i, carry):
        span = pl.ds(pl.multiple_of(i * tile, tile), tile)
        weight = wo_all[:, :, span].reshape(heads * DK, tile)
        out_ref[:, span] = jnp.dot(parts_ref[...], weight, preferred_element_type=F32).astype(BF16)
        return carry

    lax.fori_loop(0, out_ref.shape[1] // tile, mix, 0)
    for cond, make in pending:
        guarded(cond, lambda make=make: make().wait_send())


def local(tokens, beta, w_query, w_key, w_value, gain, w_out):
    rows, features = tokens.shape
    shards, heads = lax.axis_size("ctx"), lax.axis_size("head")
    depth = 4
    width = heads // depth
    model = w_query.shape[0]
    vmem, hbm = pl.BlockSpec(memory_space=pltpu.VMEM), pl.BlockSpec(memory_space=pl.ANY)
    dma = pltpu.SemaphoreType.DMA
    return pl.pallas_call(
        functools.partial(layer_kernel, shards, heads, depth),
        out_shape=jax.ShapeDtypeStruct((rows // heads, w_out.shape[1]), BF16),
        in_specs=[hbm, vmem, hbm, hbm, hbm, vmem, hbm],
        out_specs=vmem,
        scratch_shapes=[
            pltpu.VMEM((heads, rows, features), BF16),
            pltpu.VMEM((model, 3 * DK), BF16),
            pltpu.VMEM((rows, 3 * DK), F32),
            pltpu.VMEM((heads, DK, w_out.shape[1]), BF16),
            pltpu.VMEM((rows, DK), BF16),
            pltpu.VMEM((rows, DK), F32),
            pltpu.VMEM((shards, DK, 2 * DK), BF16),
            pltpu.VMEM((rows, DK), BF16),
            pltpu.VMEM((rows // heads, heads * DK), BF16),
            dma((6,)),
            dma((heads, TOKEN_PIECES)),
            dma((heads, TOKEN_PIECES)),
            dma((heads, TOKEN_PIECES)),
            dma((width - 1, heads, TOKEN_PIECES)),
            dma((heads, OUT_PIECES)),
            dma((heads, OUT_PIECES)),
            dma((heads, OUT_PIECES)),
            dma((width - 1, heads, OUT_PIECES)),
            dma((heads, 2)),
            dma((heads, 2)),
            dma((heads,)),
            dma((heads,)),
            dma((shards,)),
            dma((shards,)),
            dma((heads,)),
            dma((heads,)),
        ],
        compiler_params=pltpu.CompilerParams(
            collective_id=0, has_side_effects=True, vmem_limit_bytes=60 * 2**20
        ),
    )(tokens, beta.reshape(rows // CHUNK, CHUNK), w_query, w_key, w_value, gain.reshape(1, DK), w_out)


def solution(mesh):
    placed = (
        P("ctx", "head"),
        P("ctx", "head"),
        P(None, "head"),
        P(None, "head"),
        P(None, "head"),
        P(),
        P("head", None),
    )
    return jax.shard_map(
        local, mesh=mesh, in_specs=placed, out_specs=P(("ctx", "head"), None), check_vma=False
    )
```

```python
import functools

import jax
import jax.numpy as jnp
from jax import lax
from jax.experimental import pallas as pl
from jax.experimental.pallas import tpu as pltpu
from jax.sharding import PartitionSpec as P

DK = 128
CHUNK = 128
F32, BF16 = jnp.float32, jnp.bfloat16


def dot(left, right):
    return jnp.dot(left.astype(BF16), right.astype(BF16), preferred_element_type=F32)


def dot_nt(left, right):
    return lax.dot_general(
        left.astype(BF16), right.astype(BF16), (((1,), (1,)), ((), ())), preferred_element_type=F32
    )


def dot_tn(left, right):
    return lax.dot_general(
        left.astype(BF16), right.astype(BF16), (((0,), (0,)), ((), ())), preferred_element_type=F32
    )


def unit_silu(raw):
    act = raw / (1.0 + jnp.exp(-raw))
    return act * lax.rsqrt(jnp.sum(act * act, axis=-1, keepdims=True) + 1e-6)


def unit_lower_inverses(lowers):
    size = lowers[0].shape[0]
    row = lax.broadcasted_iota(jnp.int32, (size, size), 0)
    col = lax.broadcasted_iota(jnp.int32, (size, size), 1)
    inverses = None
    level = 0
    while (1 << level) < size:
        mask = (
            ((row >> (level + 1)) == (col >> (level + 1)))
            & (((row >> level) & 1) == 1)
            & (((col >> level) & 1) == 0)
        )
        parts = [jnp.where(mask, lower, 0.0) for lower in lowers]
        if inverses is None:
            eye = jnp.where(row == col, 1.0, 0.0)
            inverses = [eye - part for part in parts]
        else:
            halves = [dot(inverse, part) for inverse, part in zip(inverses, parts)]
            inverses = [
                inverse - dot(half, inverse) for inverse, half in zip(inverses, halves)
            ]
        level += 1
    return inverses


def shard_maps(raw, rates, emit, midway):
    count = len(raw)
    row = lax.broadcasted_iota(jnp.int32, (CHUNK, CHUNK), 0)
    col = lax.broadcasted_iota(jnp.int32, (CHUNK, CHUNK), 1)
    queries = [unit_silu(raw[i][0]) for i in range(count)]
    keys = [unit_silu(raw[i][1]) for i in range(count)]
    lowers = [
        jnp.where(row > col, rates[i] * dot_nt(keys[i], keys[i]), 0.0) for i in range(count)
    ]
    inverses = unit_lower_inverses(lowers)
    midway()
    factors = [
        dot(inverses[i], jnp.concatenate([rates[i] * keys[i], rates[i] * raw[i][2]], axis=1))
        for i in range(count)
    ]
    moves = [dot_tn(keys[i], factors[i]) for i in range(count)]
    reads = [
        dot(jnp.where(row >= col, dot_nt(queries[i], keys[i]), 0.0), factors[i])
        for i in range(count)
    ]
    zero = jnp.zeros((DK, DK), F32)
    state = jnp.concatenate([jnp.where(row == col, 1.0, 0.0), zero], axis=1)
    for i in range(count):
        from_state = dot(queries[i] - reads[i][:, :DK], state)
        emit(i, from_state[:, :DK], from_state[:, DK:] + reads[i][:, DK:])
        state = (
            state
            - dot(moves[i][:, :DK], state)
            + jnp.concatenate([zero, moves[i][:, DK:]], axis=1)
        )
    return state


class LineGather:
    def __init__(self, own, slot, pieces, early, depth, width, sems, pending):
        self.own, self.slot, self.pieces, self.early = own, slot, pieces, early
        self.depth, self.width = depth, width
        self.recv, self.up, self.down, self.cross = sems
        self.pending = pending
        me = lax.axis_index("head")
        self.z, self.x = me // width, lax.rem(me, width)

    def head(self, z, j=0):
        return z * self.width + lax.rem(self.x + j, self.width)

    def send(self, cond, source, shard, piece, sem, target):
        def make():
            return pltpu.make_async_remote_copy(
                src_ref=source,
                dst_ref=self.slot(shard, piece),
                send_sem=sem,
                recv_sem=self.recv.at[shard, piece],
                device_id={"head": target},
                device_id_type=pl.DeviceIdType.MESH,
            )

        guarded(cond, lambda: make().start())
        self.pending.append((cond, make))

    def arrive(self, shard, piece):
        view = self.slot(shard, piece)
        pltpu.make_async_copy(view, view, self.recv.at[shard, piece]).wait()

    def send_up(self, source, shard, piece):
        self.send(
            self.z < self.depth - 1, source, shard, piece, self.up.at[shard, piece], self.head(self.z + 1)
        )

    def send_down(self, source, shard, piece):
        self.send(self.z > 0, source, shard, piece, self.down.at[shard, piece], self.head(self.z - 1))

    def send_across(self, cond, source, shard, piece):
        for j in range(1, self.width):
            self.send(
                cond, source, shard, piece, self.cross.at[j - 1, shard, piece], self.head(self.z, j)
            )

    def start(self):
        me = self.head(self.z)
        for piece in range(self.pieces):
            source = self.own(piece)
            self.send_across(None, source, me, piece)
            self.send_up(source, me, piece)
            self.send_down(source, me, piece)

    def start_early(self):
        for piece in range(self.early):
            for j in range(1, self.width):
                shard = self.head(self.z, j)
                self.arrive(shard, piece)
                self.send_up(self.slot(shard, piece), shard, piece)
                self.send_down(self.slot(shard, piece), shard, piece)

    def sides(self, distance):
        below, above = self.z - distance, self.z + distance
        return (
            (below >= 0, jnp.maximum(below, 0), True),
            (above < self.depth, jnp.minimum(above, self.depth - 1), False),
        )

    def stage(self, distance):
        for piece in range(self.pieces):
            for there, source_z, upward in self.sides(distance):
                for j in range(self.width if piece < self.early else 1):
                    shard = self.head(source_z, j)
                    view = self.slot(shard, piece)
                    guarded(there, functools.partial(self.arrive, shard, piece))
                    if upward and distance < self.depth - 1:
                        self.send(
                            there & (self.z < self.depth - 1), view, shard, piece,
                            self.up.at[shard, piece], self.head(self.z + 1),
                        )
                    elif distance < self.depth - 1:
                        self.send(
                            there & (self.z > 0), view, shard, piece,
                            self.down.at[shard, piece], self.head(self.z - 1),
                        )
                if piece >= self.early:
                    shard = self.head(source_z)
                    self.send_across(there, self.slot(shard, piece), shard, piece)

    def finish(self, shard):
        for piece in range(self.early, self.pieces):
            self.arrive(shard, piece)


def guarded(cond, action):
    if cond is None:
        action()
    else:
        pl.when(cond)(action)


TOKEN_PIECES, TOKEN_EARLY = 8, 0
OUT_PIECES, OUT_EARLY = 1, 1


def layer_kernel(
    shards, heads, depth,
    tokens_ref, beta_ref, wq_ref, wk_ref, wv_ref, gain_ref, wo_ref,
    out_ref,
    x_ref, w_ref, raw_ref, wo_all, query_ref, own_ref, states_ref, normed_ref, parts_ref,
    copy_sems, tok_recv, tok_up, tok_down, tok_cross,
    wo_recv, wo_up, wo_down, wo_cross, core_send, core_recv, pair_send, pair_recv,
    state_send, state_recv, part_send, part_recv,
):
    ctx, head = lax.axis_index("ctx"), lax.axis_index("head")
    width = heads // depth
    rows, features = tokens_ref.shape
    core, pair = lax.rem(ctx, 2), lax.rem(ctx // 2, 2)
    core_partner, pair_partner = ctx + 1 - 2 * core, ctx + 2 - 4 * pair
    pending = []

    loads = [
        pltpu.make_async_copy(ref, w_ref.at[:, pl.ds(i * DK, DK)], copy_sems.at[i])
        for i, ref in enumerate((wq_ref, wk_ref, wv_ref))
    ]
    loads.append(pltpu.make_async_copy(tokens_ref, x_ref.at[head], copy_sems.at[3]))
    quarter = wo_ref.shape[0] // 4
    loads.append(pltpu.make_async_copy(wo_ref, wo_all.at[head], copy_sems.at[4]))
    for load in loads:
        load.start()

    barrier = pltpu.get_barrier_semaphore()
    for j in range(1, heads):
        pl.semaphore_signal(
            barrier, inc=1, device_id={"head": lax.rem(head + j, heads)},
            device_id_type=pl.DeviceIdType.MESH,
        )
    for j in range(1, shards):
        pl.semaphore_signal(
            barrier, inc=1, device_id={"ctx": lax.rem(ctx + j, shards)},
            device_id_type=pl.DeviceIdType.MESH,
        )
    pl.semaphore_wait(barrier, heads + shards - 2)

    piece_rows = rows // TOKEN_PIECES
    gather = LineGather(
        lambda piece: tokens_ref.at[pl.ds(piece * piece_rows, piece_rows)],
        lambda shard, piece: x_ref.at[shard, pl.ds(piece * piece_rows, piece_rows)],
        TOKEN_PIECES, TOKEN_EARLY, depth, width, (tok_recv, tok_up, tok_down, tok_cross), pending,
    )
    out_rows = quarter // OUT_PIECES

    def quarter_start(pair, core):
        return (2 * pair + core) * quarter

    def out_slot(shard, piece):
        start = pl.multiple_of(quarter_start(pair, core) + piece * out_rows, 16)
        return wo_all.at[shard, pl.ds(start, out_rows)]

    def out_own(piece):
        start = pl.multiple_of(quarter_start(pair, core) + piece * out_rows, 16)
        return wo_ref.at[pl.ds(start, out_rows)]

    def out_quarter(shard, pair, core):
        return wo_all.at[shard, pl.ds(pl.multiple_of(quarter_start(pair, core), 16), quarter)]

    spread = LineGather(
        out_own, out_slot, OUT_PIECES, OUT_EARLY, depth, width,
        (wo_recv, wo_up, wo_down, wo_cross), pending,
    )

    def hand_over(cond, view, send_sem, recv_sem, target):
        def make():
            return pltpu.make_async_remote_copy(
                src_ref=view, dst_ref=view, send_sem=send_sem, recv_sem=recv_sem,
                device_id={"ctx": target}, device_id_type=pl.DeviceIdType.MESH,
            )

        guarded(cond, lambda: make().start())
        pending.append((cond, make))

    def swap(shard, cond):
        view = out_quarter(shard, pair, core)
        hand_over(cond, view, pair_send.at[shard], pair_recv.at[shard], pair_partner)
        hand_over(cond, view, core_send.at[shard, 0], core_recv.at[shard, 0], core_partner)

    def swap_paired(shard, cond):
        view = out_quarter(shard, 1 - pair, core)
        guarded(cond, pltpu.make_async_copy(view, view, pair_recv.at[shard]).wait)
        hand_over(cond, view, core_send.at[shard, 1], core_recv.at[shard, 1], core_partner)

    def at_distance(distance, action):
        for index, (there, source_z, _) in enumerate(spread.sides(distance)):
            if distance == 0 and index:
                continue
            for j in range(0 if distance else 1, width):
                action(spread.head(source_z, j), there)

    def project(shard, first=False):
        tile = 256

        def step(i, carry):
            span = pl.ds(pl.multiple_of(i * tile, tile), tile)
            weight = w_ref[pl.ds(pl.multiple_of(shard * features, 128), features), :]
            term = jnp.dot(x_ref[shard, span, :], weight, preferred_element_type=F32)
            raw_ref[span, :] = term if first else raw_ref[span, :] + term
            return carry

        lax.fori_loop(0, rows // tile, step, 0)

    def finish_across(distance):
        for index, (there, source_z, _) in enumerate(gather.sides(distance)):
            if distance == 0 and index:
                continue
            for j in range(1, width):
                shard = gather.head(source_z, j)

                def take(shard=shard):
                    gather.finish(shard)
                    project(shard)

                guarded(there, take)

    spread.start()
    gather.start()
    for load in loads[:4]:
        load.wait()
    spread.start_early()
    at_distance(0, swap)
    gather.start_early()
    project(head, first=True)
    for distance in range(1, depth):
        gather.stage(distance)
        spread.stage(distance)
        at_distance(distance, swap)
        at_distance(distance - 1, swap_paired)
        for there, source_z, _ in gather.sides(distance):
            guarded(there, functools.partial(project, gather.head(source_z)))
        finish_across(distance - 1)
    finish_across(depth - 1)
    loads[4].wait()

    def midway():
        at_distance(depth - 1, swap_paired)

    def emit(i, query, own):
        span = pl.ds(i * CHUNK, CHUNK)
        query_ref[span, :] = query.astype(BF16)
        own_ref[span, :] = own

    raw = [
        [raw_ref[pl.ds(i * CHUNK, CHUNK), pl.ds(j * DK, DK)] for j in range(3)]
        for i in range(rows // CHUNK)
    ]
    rate_columns = beta_ref[...].T
    rates = [rate_columns[:, i : i + 1] for i in range(rows // CHUNK)]
    states_ref[ctx] = shard_maps(raw, rates, emit, midway).astype(BF16)

    for other in range(1, shards):
        def make(other=other):
            return pltpu.make_async_remote_copy(
                src_ref=states_ref.at[ctx], dst_ref=states_ref.at[ctx],
                send_sem=state_send.at[other], recv_sem=state_recv.at[ctx],
                device_id={"ctx": jnp.int32(other)}, device_id_type=pl.DeviceIdType.MESH,
            )

        guarded(ctx < other, lambda make=make: make().start())
        pending.append((ctx < other, make))

    for shard in range(shards - 1):
        @pl.when(shard < ctx)
        def _(shard=shard):
            view = states_ref.at[shard]
            pltpu.make_async_copy(view, view, state_recv.at[shard]).wait()

        @pl.when(shard >= ctx)
        def _(shard=shard):
            @pl.when(shard > ctx)
            def _():
                states_ref[shard] = jnp.zeros(states_ref.shape[1:], BF16)

    start = jnp.zeros((DK, DK), F32)
    for shard in range(shards - 1):
        state = states_ref[shard]
        after = dot(state[:, :DK], start) + state[:, DK:].astype(F32)
        start = jnp.where(shard < ctx, after, start)
    block = rows // heads
    for i in range(rows // CHUNK):
        span = pl.ds(i * CHUNK, CHUNK)
        recurrent = own_ref[span, :] + dot(query_ref[span, :], start)
        scale = lax.rsqrt(jnp.mean(recurrent * recurrent, axis=-1, keepdims=True) + 1e-5)
        normed_ref[span, :] = (recurrent * scale * gain_ref[...]).astype(BF16)

    mine = pl.multiple_of(head * DK, DK)
    own_part = pltpu.make_async_copy(
        normed_ref.at[pl.ds(pl.multiple_of(head * block, 16), block)],
        parts_ref.at[:, pl.ds(mine, DK)], copy_sems.at[5],
    )
    own_part.start()
    for j in range(1, heads):
        other = lax.rem(head + j, heads)

        def make(other=other, j=j):
            return pltpu.make_async_remote_copy(
                src_ref=normed_ref.at[pl.ds(pl.multiple_of(other * block, 16), block)],
                dst_ref=parts_ref.at[:, pl.ds(mine, DK)],
                send_sem=part_send.at[j], recv_sem=part_recv.at[j],
                device_id={"head": other}, device_id_type=pl.DeviceIdType.MESH,
            )

        make().start()
        pending.append((None, make))

    for j in range(1, heads):
        source = lax.rem(head + heads - j, heads)
        view = parts_ref.at[:, pl.ds(pl.multiple_of(source * DK, DK), DK)]
        pltpu.make_async_copy(view, view, part_recv.at[j]).wait()
    own_part.wait()
    for j in range(1, heads):
        shard = lax.rem(head + j, heads)
        for index, from_pair in enumerate((pair, 1 - pair)):
            view = out_quarter(shard, from_pair, 1 - core)
            pltpu.make_async_copy(view, view, core_recv.at[shard, index]).wait()

    tile = 512

    def mix(i, carry):
        span = pl.ds(pl.multiple_of(i * tile, tile), tile)
        weight = wo_all[:, :, span].reshape(heads * DK, tile)
        out_ref[:, span] = jnp.dot(parts_ref[...], weight, preferred_element_type=F32).astype(BF16)
        return carry

    lax.fori_loop(0, out_ref.shape[1] // tile, mix, 0)
    for cond, make in pending:
        guarded(cond, lambda make=make: make().wait_send())


def local(tokens, beta, w_query, w_key, w_value, gain, w_out):
    rows, features = tokens.shape
    shards, heads = lax.axis_size("ctx"), lax.axis_size("head")
    depth = 4
    width = heads // depth
    model = w_query.shape[0]
    vmem, hbm = pl.BlockSpec(memory_space=pltpu.VMEM), pl.BlockSpec(memory_space=pl.ANY)
    dma = pltpu.SemaphoreType.DMA
    return pl.pallas_call(
        functools.partial(layer_kernel, shards, heads, depth),
        out_shape=jax.ShapeDtypeStruct((rows // heads, w_out.shape[1]), BF16),
        in_specs=[hbm, vmem, hbm, hbm, hbm, vmem, hbm],
        out_specs=vmem,
        scratch_shapes=[
            pltpu.VMEM((heads, rows, features), BF16),
            pltpu.VMEM((model, 3 * DK), BF16),
            pltpu.VMEM((rows, 3 * DK), F32),
            pltpu.VMEM((heads, DK, w_out.shape[1]), BF16),
            pltpu.VMEM((rows, DK), BF16),
            pltpu.VMEM((rows, DK), F32),
            pltpu.VMEM((shards, DK, 2 * DK), BF16),
            pltpu.VMEM((rows, DK), BF16),
            pltpu.VMEM((rows // heads, heads * DK), BF16),
            dma((6,)),
            dma((heads, TOKEN_PIECES)),
            dma((heads, TOKEN_PIECES)),
            dma((heads, TOKEN_PIECES)),
            dma((width - 1, heads, TOKEN_PIECES)),
            dma((heads, OUT_PIECES)),
            dma((heads, OUT_PIECES)),
            dma((heads, OUT_PIECES)),
            dma((width - 1, heads, OUT_PIECES)),
            dma((heads, 2)),
            dma((heads, 2)),
            dma((heads,)),
            dma((heads,)),
            dma((shards,)),
            dma((shards,)),
            dma((heads,)),
            dma((heads,)),
        ],
        compiler_params=pltpu.CompilerParams(
            collective_id=0, has_side_effects=True, vmem_limit_bytes=60 * 2**20
        ),
    )(tokens, beta.reshape(rows // CHUNK, CHUNK), w_query, w_key, w_value, gain.reshape(1, DK), w_out)


def solution(mesh):
    placed = (
        P("ctx", "head"),
        P("ctx", "head"),
        P(None, "head"),
        P(None, "head"),
        P(None, "head"),
        P(),
        P("head", None),
    )
    return jax.shard_map(
        local, mesh=mesh, in_specs=placed, out_specs=P(("ctx", "head"), None), check_vma=False
    )
```

```python
import functools

import jax
import jax.numpy as jnp
from jax import lax
from jax.experimental import pallas as pl
from jax.experimental.pallas import tpu as pltpu
from jax.sharding import PartitionSpec as P

DK = 128
CHUNK = 128
F32, BF16 = jnp.float32, jnp.bfloat16


def dot(left, right):
    return jnp.dot(left.astype(BF16), right.astype(BF16), preferred_element_type=F32)


def dot_nt(left, right):
    return lax.dot_general(
        left.astype(BF16), right.astype(BF16), (((1,), (1,)), ((), ())), preferred_element_type=F32
    )


def dot_tn(left, right):
    return lax.dot_general(
        left.astype(BF16), right.astype(BF16), (((0,), (0,)), ((), ())), preferred_element_type=F32
    )


def unit_silu(raw):
    act = raw / (1.0 + jnp.exp(-raw))
    return act * lax.rsqrt(jnp.sum(act * act, axis=-1, keepdims=True) + 1e-6)


def unit_lower_inverses(lowers):
    size = lowers[0].shape[0]
    row = lax.broadcasted_iota(jnp.int32, (size, size), 0)
    col = lax.broadcasted_iota(jnp.int32, (size, size), 1)
    inverses = None
    level = 0
    while (1 << level) < size:
        mask = (
            ((row >> (level + 1)) == (col >> (level + 1)))
            & (((row >> level) & 1) == 1)
            & (((col >> level) & 1) == 0)
        )
        parts = [jnp.where(mask, lower, 0.0) for lower in lowers]
        if inverses is None:
            eye = jnp.where(row == col, 1.0, 0.0)
            inverses = [eye - part for part in parts]
        else:
            halves = [dot(inverse, part) for inverse, part in zip(inverses, parts)]
            inverses = [
                inverse - dot(half, inverse) for inverse, half in zip(inverses, halves)
            ]
        level += 1
    return inverses


def shard_maps(raw, rates, emit, midway):
    count = len(raw)
    row = lax.broadcasted_iota(jnp.int32, (CHUNK, CHUNK), 0)
    col = lax.broadcasted_iota(jnp.int32, (CHUNK, CHUNK), 1)
    queries = [unit_silu(raw[i][0]) for i in range(count)]
    keys = [unit_silu(raw[i][1]) for i in range(count)]
    lowers = [
        jnp.where(row > col, rates[i] * dot_nt(keys[i], keys[i]), 0.0) for i in range(count)
    ]
    inverses = unit_lower_inverses(lowers)
    midway()
    factors = [
        dot(inverses[i], jnp.concatenate([rates[i] * keys[i], rates[i] * raw[i][2]], axis=1))
        for i in range(count)
    ]
    moves = [dot_tn(keys[i], factors[i]) for i in range(count)]
    reads = [
        dot(jnp.where(row >= col, dot_nt(queries[i], keys[i]), 0.0), factors[i])
        for i in range(count)
    ]
    zero = jnp.zeros((DK, DK), F32)
    state = jnp.concatenate([jnp.where(row == col, 1.0, 0.0), zero], axis=1)
    for i in range(count):
        from_state = dot(queries[i] - reads[i][:, :DK], state)
        emit(i, from_state[:, :DK], from_state[:, DK:] + reads[i][:, DK:])
        state = (
            state
            - dot(moves[i][:, :DK], state)
            + jnp.concatenate([zero, moves[i][:, DK:]], axis=1)
        )
    return state


class LineGather:
    def __init__(self, own, slot, pieces, early, depth, width, sems, pending):
        self.own, self.slot, self.pieces, self.early = own, slot, pieces, early
        self.depth, self.width = depth, width
        self.recv, self.up, self.down, self.cross = sems
        self.pending = pending
        me = lax.axis_index("head")
        self.z, self.x = me // width, lax.rem(me, width)

    def head(self, z, j=0):
        return z * self.width + lax.rem(self.x + j, self.width)

    def send(self, cond, source, shard, piece, sem, target):
        def make():
            return pltpu.make_async_remote_copy(
                src_ref=source,
                dst_ref=self.slot(shard, piece),
                send_sem=sem,
                recv_sem=self.recv.at[shard, piece],
                device_id={"head": target},
                device_id_type=pl.DeviceIdType.MESH,
            )

        guarded(cond, lambda: make().start())
        self.pending.append((cond, make))

    def arrive(self, shard, piece):
        view = self.slot(shard, piece)
        pltpu.make_async_copy(view, view, self.recv.at[shard, piece]).wait()

    def send_up(self, source, shard, piece):
        self.send(
            self.z < self.depth - 1, source, shard, piece, self.up.at[shard, piece], self.head(self.z + 1)
        )

    def send_down(self, source, shard, piece):
        self.send(self.z > 0, source, shard, piece, self.down.at[shard, piece], self.head(self.z - 1))

    def send_across(self, cond, source, shard, piece):
        for j in range(1, self.width):
            self.send(
                cond, source, shard, piece, self.cross.at[j - 1, shard, piece], self.head(self.z, j)
            )

    def start(self):
        me = self.head(self.z)
        for piece in range(self.pieces):
            source = self.own(piece)
            self.send_across(None, source, me, piece)
            self.send_up(source, me, piece)
            self.send_down(source, me, piece)

    def start_early(self):
        for piece in range(self.early):
            for j in range(1, self.width):
                shard = self.head(self.z, j)
                self.arrive(shard, piece)
                self.send_up(self.slot(shard, piece), shard, piece)
                self.send_down(self.slot(shard, piece), shard, piece)

    def sides(self, distance):
        below, above = self.z - distance, self.z + distance
        return (
            (below >= 0, jnp.maximum(below, 0), True),
            (above < self.depth, jnp.minimum(above, self.depth - 1), False),
        )

    def stage(self, distance):
        for piece in range(self.pieces):
            for there, source_z, upward in self.sides(distance):
                for j in range(self.width if piece < self.early else 1):
                    shard = self.head(source_z, j)
                    view = self.slot(shard, piece)
                    guarded(there, functools.partial(self.arrive, shard, piece))
                    if upward and distance < self.depth - 1:
                        self.send(
                            there & (self.z < self.depth - 1), view, shard, piece,
                            self.up.at[shard, piece], self.head(self.z + 1),
                        )
                    elif distance < self.depth - 1:
                        self.send(
                            there & (self.z > 0), view, shard, piece,
                            self.down.at[shard, piece], self.head(self.z - 1),
                        )
                if piece >= self.early:
                    shard = self.head(source_z)
                    self.send_across(there, self.slot(shard, piece), shard, piece)

    def finish(self, shard):
        for piece in range(self.early, self.pieces):
            self.arrive(shard, piece)


def guarded(cond, action):
    if cond is None:
        action()
    else:
        pl.when(cond)(action)


TOKEN_PIECES, TOKEN_EARLY = 4, 0
OUT_PIECES, OUT_EARLY = 1, 1


def layer_kernel(
    shards, heads, depth,
    tokens_ref, beta_ref, wq_ref, wk_ref, wv_ref, gain_ref, wo_ref,
    out_ref,
    x_ref, w_ref, raw_ref, wo_all, query_ref, own_ref, states_ref, normed_ref, parts_ref,
    copy_sems, tok_recv, tok_up, tok_down, tok_cross,
    wo_recv, wo_up, wo_down, wo_cross, core_send, core_recv, pair_send, pair_recv,
    state_send, state_recv, part_send, part_recv,
):
    ctx, head = lax.axis_index("ctx"), lax.axis_index("head")
    width = heads // depth
    rows, features = tokens_ref.shape
    core, pair = lax.rem(ctx, 2), lax.rem(ctx // 2, 2)
    core_partner, pair_partner = ctx + 1 - 2 * core, ctx + 2 - 4 * pair
    pending = []

    loads = [
        pltpu.make_async_copy(ref, w_ref.at[:, pl.ds(i * DK, DK)], copy_sems.at[i])
        for i, ref in enumerate((wq_ref, wk_ref, wv_ref))
    ]
    loads.append(pltpu.make_async_copy(tokens_ref, x_ref.at[head], copy_sems.at[3]))
    quarter = wo_ref.shape[0] // 4
    loads.append(pltpu.make_async_copy(wo_ref, wo_all.at[head], copy_sems.at[4]))
    for load in loads:
        load.start()

    barrier = pltpu.get_barrier_semaphore()
    for j in range(1, heads):
        pl.semaphore_signal(
            barrier, inc=1, device_id={"head": lax.rem(head + j, heads)},
            device_id_type=pl.DeviceIdType.MESH,
        )
    for j in range(1, shards):
        pl.semaphore_signal(
            barrier, inc=1, device_id={"ctx": lax.rem(ctx + j, shards)},
            device_id_type=pl.DeviceIdType.MESH,
        )
    pl.semaphore_wait(barrier, heads + shards - 2)

    piece_rows = rows // TOKEN_PIECES
    gather = LineGather(
        lambda piece: tokens_ref.at[pl.ds(piece * piece_rows, piece_rows)],
        lambda shard, piece: x_ref.at[shard, pl.ds(piece * piece_rows, piece_rows)],
        TOKEN_PIECES, TOKEN_EARLY, depth, width, (tok_recv, tok_up, tok_down, tok_cross), pending,
    )
    out_rows = quarter // OUT_PIECES

    def quarter_start(pair, core):
        return (2 * pair + core) * quarter

    def out_slot(shard, piece):
        start = pl.multiple_of(quarter_start(pair, core) + piece * out_rows, 16)
        return wo_all.at[shard, pl.ds(start, out_rows)]

    def out_own(piece):
        start = pl.multiple_of(quarter_start(pair, core) + piece * out_rows, 16)
        return wo_ref.at[pl.ds(start, out_rows)]

    def out_quarter(shard, pair, core):
        return wo_all.at[shard, pl.ds(pl.multiple_of(quarter_start(pair, core), 16), quarter)]

    spread = LineGather(
        out_own, out_slot, OUT_PIECES, OUT_EARLY, depth, width,
        (wo_recv, wo_up, wo_down, wo_cross), pending,
    )

    def hand_over(cond, view, send_sem, recv_sem, target):
        def make():
            return pltpu.make_async_remote_copy(
                src_ref=view, dst_ref=view, send_sem=send_sem, recv_sem=recv_sem,
                device_id={"ctx": target}, device_id_type=pl.DeviceIdType.MESH,
            )

        guarded(cond, lambda: make().start())
        pending.append((cond, make))

    def swap(shard, cond):
        view = out_quarter(shard, pair, core)
        hand_over(cond, view, pair_send.at[shard], pair_recv.at[shard], pair_partner)
        hand_over(cond, view, core_send.at[shard, 0], core_recv.at[shard, 0], core_partner)

    def swap_paired(shard, cond):
        view = out_quarter(shard, 1 - pair, core)
        guarded(cond, pltpu.make_async_copy(view, view, pair_recv.at[shard]).wait)
        hand_over(cond, view, core_send.at[shard, 1], core_recv.at[shard, 1], core_partner)

    def at_distance(distance, action):
        for index, (there, source_z, _) in enumerate(spread.sides(distance)):
            if distance == 0 and index:
                continue
            for j in range(0 if distance else 1, width):
                action(spread.head(source_z, j), there)

    def project(shard, first=False):
        tile = 256

        def step(i, carry):
            span = pl.ds(pl.multiple_of(i * tile, tile), tile)
            weight = w_ref[pl.ds(pl.multiple_of(shard * features, 128), features), :]
            term = jnp.dot(x_ref[shard, span, :], weight, preferred_element_type=F32)
            raw_ref[span, :] = term if first else raw_ref[span, :] + term
            return carry

        lax.fori_loop(0, rows // tile, step, 0)

    def finish_across(distance):
        for index, (there, source_z, _) in enumerate(gather.sides(distance)):
            if distance == 0 and index:
                continue
            for j in range(1, width):
                shard = gather.head(source_z, j)

                def take(shard=shard):
                    gather.finish(shard)
                    project(shard)

                guarded(there, take)

    spread.start()
    gather.start()
    for load in loads[:4]:
        load.wait()
    spread.start_early()
    at_distance(0, swap)
    gather.start_early()
    project(head, first=True)
    for distance in range(1, depth):
        gather.stage(distance)
        if distance > 1:
            spread.stage(distance - 1)
            at_distance(distance - 1, swap)
            at_distance(distance - 2, swap_paired)
        for there, source_z, _ in gather.sides(distance):
            guarded(there, functools.partial(project, gather.head(source_z)))
        finish_across(distance - 1)
    finish_across(depth - 1)
    loads[4].wait()

    def midway():
        spread.stage(depth - 1)
        at_distance(depth - 1, swap)
        at_distance(depth - 2, swap_paired)

    def emit(i, query, own):
        span = pl.ds(i * CHUNK, CHUNK)
        query_ref[span, :] = query.astype(BF16)
        own_ref[span, :] = own

    raw = [
        [raw_ref[pl.ds(i * CHUNK, CHUNK), pl.ds(j * DK, DK)] for j in range(3)]
        for i in range(rows // CHUNK)
    ]
    rate_columns = beta_ref[...].T
    rates = [rate_columns[:, i : i + 1] for i in range(rows // CHUNK)]
    states_ref[ctx] = shard_maps(raw, rates, emit, midway).astype(BF16)

    for other in range(1, shards):
        def make(other=other):
            return pltpu.make_async_remote_copy(
                src_ref=states_ref.at[ctx], dst_ref=states_ref.at[ctx],
                send_sem=state_send.at[other], recv_sem=state_recv.at[ctx],
                device_id={"ctx": jnp.int32(other)}, device_id_type=pl.DeviceIdType.MESH,
            )

        guarded(ctx < other, lambda make=make: make().start())
        pending.append((ctx < other, make))

    for shard in range(shards - 1):
        @pl.when(shard < ctx)
        def _(shard=shard):
            view = states_ref.at[shard]
            pltpu.make_async_copy(view, view, state_recv.at[shard]).wait()

        @pl.when(shard >= ctx)
        def _(shard=shard):
            @pl.when(shard > ctx)
            def _():
                states_ref[shard] = jnp.zeros(states_ref.shape[1:], BF16)

    start = jnp.zeros((DK, DK), F32)
    for shard in range(shards - 1):
        state = states_ref[shard]
        after = dot(state[:, :DK], start) + state[:, DK:].astype(F32)
        start = jnp.where(shard < ctx, after, start)
    block = rows // heads
    for i in range(rows // CHUNK):
        span = pl.ds(i * CHUNK, CHUNK)
        recurrent = own_ref[span, :] + dot(query_ref[span, :], start)
        scale = lax.rsqrt(jnp.mean(recurrent * recurrent, axis=-1, keepdims=True) + 1e-5)
        normed_ref[span, :] = (recurrent * scale * gain_ref[...]).astype(BF16)

    mine = pl.multiple_of(head * DK, DK)
    own_part = pltpu.make_async_copy(
        normed_ref.at[pl.ds(pl.multiple_of(head * block, 16), block)],
        parts_ref.at[:, pl.ds(mine, DK)], copy_sems.at[5],
    )
    own_part.start()
    for j in range(1, heads):
        other = lax.rem(head + j, heads)

        def make(other=other, j=j):
            return pltpu.make_async_remote_copy(
                src_ref=normed_ref.at[pl.ds(pl.multiple_of(other * block, 16), block)],
                dst_ref=parts_ref.at[:, pl.ds(mine, DK)],
                send_sem=part_send.at[j], recv_sem=part_recv.at[j],
                device_id={"head": other}, device_id_type=pl.DeviceIdType.MESH,
            )

        make().start()
        pending.append((None, make))

    at_distance(depth - 1, swap_paired)
    for j in range(1, heads):
        source = lax.rem(head + heads - j, heads)
        view = parts_ref.at[:, pl.ds(pl.multiple_of(source * DK, DK), DK)]
        pltpu.make_async_copy(view, view, part_recv.at[j]).wait()
    own_part.wait()
    for j in range(1, heads):
        shard = lax.rem(head + j, heads)
        for index, from_pair in enumerate((pair, 1 - pair)):
            view = out_quarter(shard, from_pair, 1 - core)
            pltpu.make_async_copy(view, view, core_recv.at[shard, index]).wait()

    tile = 512

    def mix(i, carry):
        span = pl.ds(pl.multiple_of(i * tile, tile), tile)
        weight = wo_all[:, :, span].reshape(heads * DK, tile)
        out_ref[:, span] = jnp.dot(parts_ref[...], weight, preferred_element_type=F32).astype(BF16)
        return carry

    lax.fori_loop(0, out_ref.shape[1] // tile, mix, 0)
    for cond, make in pending:
        guarded(cond, lambda make=make: make().wait_send())


def local(tokens, beta, w_query, w_key, w_value, gain, w_out):
    rows, features = tokens.shape
    shards, heads = lax.axis_size("ctx"), lax.axis_size("head")
    depth = 4
    width = heads // depth
    model = w_query.shape[0]
    vmem, hbm = pl.BlockSpec(memory_space=pltpu.VMEM), pl.BlockSpec(memory_space=pl.ANY)
    dma = pltpu.SemaphoreType.DMA
    return pl.pallas_call(
        functools.partial(layer_kernel, shards, heads, depth),
        out_shape=jax.ShapeDtypeStruct((rows // heads, w_out.shape[1]), BF16),
        in_specs=[hbm, vmem, hbm, hbm, hbm, vmem, hbm],
        out_specs=vmem,
        scratch_shapes=[
            pltpu.VMEM((heads, rows, features), BF16),
            pltpu.VMEM((model, 3 * DK), BF16),
            pltpu.VMEM((rows, 3 * DK), F32),
            pltpu.VMEM((heads, DK, w_out.shape[1]), BF16),
            pltpu.VMEM((rows, DK), BF16),
            pltpu.VMEM((rows, DK), F32),
            pltpu.VMEM((shards, DK, 2 * DK), BF16),
            pltpu.VMEM((rows, DK), BF16),
            pltpu.VMEM((rows // heads, heads * DK), BF16),
            dma((6,)),
            dma((heads, TOKEN_PIECES)),
            dma((heads, TOKEN_PIECES)),
            dma((heads, TOKEN_PIECES)),
            dma((width - 1, heads, TOKEN_PIECES)),
            dma((heads, OUT_PIECES)),
            dma((heads, OUT_PIECES)),
            dma((heads, OUT_PIECES)),
            dma((width - 1, heads, OUT_PIECES)),
            dma((heads, 2)),
            dma((heads, 2)),
            dma((heads,)),
            dma((heads,)),
            dma((shards,)),
            dma((shards,)),
            dma((heads,)),
            dma((heads,)),
        ],
        compiler_params=pltpu.CompilerParams(
            collective_id=0, has_side_effects=True, vmem_limit_bytes=60 * 2**20
        ),
    )(tokens, beta.reshape(rows // CHUNK, CHUNK), w_query, w_key, w_value, gain.reshape(1, DK), w_out)


def solution(mesh):
    placed = (
        P("ctx", "head"),
        P("ctx", "head"),
        P(None, "head"),
        P(None, "head"),
        P(None, "head"),
        P(),
        P("head", None),
    )
    return jax.shard_map(
        local, mesh=mesh, in_specs=placed, out_specs=P(("ctx", "head"), None), check_vma=False
    )
```
